32 devices in a mesh: edges: 8 (over z, y), rep: 4 (over x, core).
Axes of the slice: x: 2, y: 2, z: 4, core: 2. Of those that a mesh axis runs over, the one named last changes fastest.
Arguments:
- node_latent: bfloat16 [16384, 128], P('edges'), may hold values from -6 to 6
- edge_latent: bfloat16 [327680, 128], P(('edges', 'rep')), may hold values from -6 to 6
- senders: int32 [327680], P(('edges', 'rep')), may hold values from 0 to 16383, as said below
- receivers: int32 [327680], P(('edges', 'rep')), may hold values from 0 to 16383, as said below
- edge_mask: int32 [327680], P(('edges', 'rep')), may hold values 0 or 1
- particle_mask: int32 [16384], P('edges'), may hold values 0 or 1
- edge_lift: bfloat16 [384, 128], replicated, may hold values from -0.3125 to 0.3125
- lifting: bfloat16 [128], replicated, may hold values from -3 to 3
- edge_middle: bfloat16 [128, 128], replicated, may hold values from -0.5 to 0.5
- mixing: bfloat16 [128], replicated, may hold values from -3 to 3
- edge_final: bfloat16 [128, 128], replicated, may hold values from -0.5 to 0.5
- closing: bfloat16 [128], replicated, may hold values from -3 to 3
- stretch: bfloat16 [128], replicated, may hold values from 0.099609375 to 1.8984375
- offset: bfloat16 [128], replicated, may hold values from -3 to 3
- node_first: bfloat16 [256, 128], replicated, may hold values from -0.375 to 0.375
- opening: bfloat16 [128], replicated, may hold values from -3 to 3
- node_second: bfloat16 [128, 128], replicated, may hold values from -0.5 to 0.5
- turning: bfloat16 [128], replicated, may hold values from -3 to 3
- node_third: bfloat16 [128, 128], replicated, may hold values from -0.5 to 0.5
- ending: bfloat16 [128], replicated, may hold values from -3 to 3
- dilate: bfloat16 [128], replicated, may hold values from 0.099609375 to 1.8984375
- displace: bfloat16 [128], replicated, may hold values from -3 to 3
- node_cotangent: float32 [16384, 128], P('edges'), may hold values from -6 to 6
- edge_cotangent: float32 [327680, 128], P(('edges', 'rep')), may hold values from -6 to 6
Outputs:
- node_output: float32 [16384, 128], P('edges')
- edge_output: float32 [327680, 128], P(('edges', 'rep'))
- node_grad: float32 [16384, 128], P('edges')
- edge_grad: float32 [327680, 128], P(('edges', 'rep'))
- lift_grad: float32 [384, 128], replicated
- lifting_grad: float32 [128], replicated
- middle_grad: float32 [128, 128], replicated
- mixing_grad: float32 [128], replicated
- final_grad: float32 [128, 128], replicated
- closing_grad: float32 [128], replicated
- stretch_grad: float32 [128], replicated
- offset_grad: float32 [128], replicated
- first_grad: float32 [256, 128], replicated
- opening_grad: float32 [128], replicated
- second_grad: float32 [128, 128], replicated
- turning_grad: float32 [128], replicated
- third_grad: float32 [128, 128], replicated
- ending_grad: float32 [128], replicated
- dilate_grad: float32 [128], replicated
- displace_grad: float32 [128], replicated
The draws below stay inside these ranges and needn't reach their ends.
Inputs may be any that keep to these rules, and one draw needn't show every extreme that they name: receivers[e] lies in the particle block e // 40960 of 2048 rows, that is the block of the index of edges that holds edge e. |senders[e] - receivers[e]| <= 2048 for every edge, reached in every draw.
All inputs are finite; a program needn't handle non-finite values. No bound on the sum of `edge_mask` or of `particle_mask` on one device may be relied on, other than what follows from the above.
Results may differ from the reference program's by a relative error of at most 0.009.
The reference program's roundings to bfloat16 on the way count: a program that leaves them out, or rounds other values in their place, can miss the bound.
Values may be sent and summed in bfloat16 or wider, within the bound.
A program may use at most 128 MiB of HBM per device.

```python
import jax
import jax.numpy as jnp
from jax import lax

LAT = 128
NODE_BLK = 2048
NODES = 16384
EDGES = 327680


def endpoints(key):
    group_rows = EDGES * NODE_BLK // NODES
    positions = jnp.arange(EDGES, dtype=jnp.int32)
    group = positions // group_rows
    within = jax.random.randint(jax.random.fold_in(key, 11), (EDGES,), 0, NODE_BLK)
    receiver = group * NODE_BLK + within
    offsets = jax.random.randint(jax.random.fold_in(key, 12), (EDGES,), -NODE_BLK, NODE_BLK + 1)
    leading = positions % group_rows == 0
    forced = jnp.where(receiver + NODE_BLK < NODES, NODE_BLK, -NODE_BLK)
    offsets = jnp.where(leading, forced, offsets)
    sender = jnp.clip(receiver + offsets, 0, NODES - 1)
    return (sender.astype(jnp.int32), receiver.astype(jnp.int32))


def draw_senders(key, part):
    return endpoints(key)[0]


def draw_receivers(key, part):
    return endpoints(key)[1]


def touch_ends(values, rng, smallest, high):
    spot = [jax.random.randint(jax.random.fold_in(rng, axis), (), 0, length) for axis, length in enumerate(values.shape)]
    main_axis = values.shape.index(max(values.shape))
    beside = spot[:main_axis] + [(spot[main_axis] + 1) % values.shape[main_axis]] + spot[main_axis + 1:]
    return values.at[tuple(spot)].set(smallest).at[tuple(beside)].set(high)


def steps_of(stream_key, dims, pieces, least, top_value):
    level = 1.0
    for dim, parts in pieces:
        draws = jax.random.uniform(jax.random.fold_in(jax.random.fold_in(stream_key, 6), dim), (parts,), jnp.float32, least / len(pieces), top_value / len(pieces))
        level = level * jnp.repeat(jnp.exp(draws), dims[dim] // parts).reshape((-1,) + (1,) * (len(dims) - 1 - dim))
    return level


def centred(key, dims, width, reach, shards=(), kind=jnp.bfloat16):
    drawn = width * jax.random.normal(key, dims, jnp.float32)
    if shards:
        drawn = drawn * steps_of(key, dims, shards, -0.22, 0.18)
    return jnp.clip(drawn, -reach, reach).astype(kind)


def setup_inputs(seed: int = 0) -> dict:
    keys = jax.random.split(jax.random.key(seed), 25)
    return {
        "node_latent": centred(keys[0], (NODES, LAT), 1.0, 6.0, ((0, 8),)),
        "edge_latent": centred(keys[1], (EDGES, LAT), 1.0, 6.0, ((0, 32),)),
        "senders": draw_senders(jax.random.fold_in(keys[24], 71), 0),
        "receivers": draw_receivers(jax.random.fold_in(keys[24], 71), 0),
        "edge_mask": touch_ends((jax.random.randint(keys[4], (EDGES,), 0, 20) < 17).astype(jnp.int32), jax.random.fold_in(keys[4], 1), 0, 1),
        "particle_mask": touch_ends((jax.random.randint(keys[5], (NODES,), 0, 10) < 9).astype(jnp.int32), jax.random.fold_in(keys[5], 1), 0, 1),
        "edge_lift": centred(keys[6], (3 * LAT, LAT), (3 * LAT) ** -0.5, 0.3125),
        "lifting": centred(keys[7], (LAT,), 0.5, 3.0),
        "edge_middle": centred(keys[8], (LAT, LAT), LAT ** -0.5, 0.5),
        "mixing": centred(keys[9], (LAT,), 0.5, 3.0),
        "edge_final": centred(keys[10], (LAT, LAT), LAT ** -0.5, 0.5),
        "closing": centred(keys[11], (LAT,), 0.5, 3.0),
        "stretch": jnp.clip(1.0 + 0.18 * jax.random.normal(keys[12], (LAT,), jnp.float32), 0.099609375, 1.8984375).astype(jnp.bfloat16),
        "offset": centred(keys[13], (LAT,), 0.5, 3.0),
        "node_first": centred(keys[14], (2 * LAT, LAT), (2 * LAT) ** -0.5, 0.375),
        "opening": centred(keys[15], (LAT,), 0.5, 3.0),
        "node_second": centred(keys[16], (LAT, LAT), LAT ** -0.5, 0.5),
        "turning": centred(keys[17], (LAT,), 0.5, 3.0),
        "node_third": centred(keys[18], (LAT, LAT), LAT ** -0.5, 0.5),
        "ending": centred(keys[19], (LAT,), 0.5, 3.0),
        "dilate": jnp.clip(1.0 + 0.18 * jax.random.normal(keys[20], (LAT,), jnp.float32), 0.099609375, 1.8984375).astype(jnp.bfloat16),
        "displace": centred(keys[21], (LAT,), 0.5, 3.0),
        "node_cotangent": centred(keys[22], (NODES, LAT), 1.0, 6.0, ((0, 8),), jnp.float32),
        "edge_cotangent": centred(keys[23], (EDGES, LAT), 1.0, 6.0, ((0, 32),), jnp.float32),
    }


EPSILON = 1e-05

@jax.custom_vjp
def low(v):
    return lax.optimization_barrier(v.astype(jnp.bfloat16)).astype(jnp.float32)

@jax.custom_vjp
def low_back(v):
    return v

def low_keep(v):
    return (low(v), None)

def low_pass(kept, grad):
    return (grad,)

def back_keep(v):
    return (v, None)

def back_low(kept, grad):
    return (low(grad),)
low.defvjp(low_keep, low_pass)
low_back.defvjp(back_keep, back_low)

def product(left, right):
    return jnp.dot(left, right, precision=lax.Precision.HIGHEST)

def layer_norm(values, gain_row, shift_row):
    center = values - lax.optimization_barrier(jnp.mean(values, axis=1, keepdims=True))
    factor = lax.rsqrt(lax.optimization_barrier(jnp.mean(center * center, axis=1, keepdims=True)) + EPSILON)
    return center * factor * gain_row + shift_row

def perceptron(inputs, lift_matrix, lift_bias, middle, middle_bias, final_matrix, final_bias):
    first_pre = low_back(product(inputs, lift_matrix) + lift_bias)
    hidden = low(jax.nn.silu(first_pre))
    second_pre = low_back(product(hidden, middle) + middle_bias)
    hidden = low(jax.nn.silu(second_pre))
    return low_back(product(hidden, final_matrix) + final_bias)

def reference(node_latent, edge_latent, senders, receivers, edge_mask, particle_mask, edge_lift, lifting, edge_middle, mixing, edge_final, closing, stretch, offset, node_first, opening, node_second, turning, node_third, ending, dilate, displace, node_cotangent, edge_cotangent):
    params = tuple((weight.astype(jnp.float32) for weight in (edge_lift, lifting, edge_middle, mixing, edge_final, closing, stretch, offset, node_first, opening, node_second, turning, node_third, ending, dilate, displace)))
    edge_keep = edge_mask.astype(jnp.float32)[:, None]
    particle_keep = particle_mask.astype(jnp.float32)[:, None]

    def forward(node_float, edge_float, weights):
        sent = low_back(jnp.take(node_float, senders, axis=0))
        got = low_back(jnp.take(node_float, receivers, axis=0))
        edge_in = jnp.concatenate([edge_float, sent, got], axis=1)
        edge_pre = perceptron(edge_in, *weights[0:6])
        message = layer_norm(edge_pre, weights[6], weights[7]) * edge_keep
        edge_out = edge_float + message
        summed = jax.ops.segment_sum(low(message), receivers, num_segments=NODES)
        node_in = jnp.concatenate([node_float, low(summed)], axis=1)
        node_pre = perceptron(node_in, *weights[8:14])
        node_out = node_float + particle_keep * layer_norm(node_pre, weights[14], weights[15])
        return (node_out, edge_out)
    outputs, pullback = jax.vjp(forward, node_latent.astype(jnp.float32), edge_latent.astype(jnp.float32), params)
    node_grad, edge_grad, grads = pullback((node_cotangent, edge_cotangent))
    return (outputs[0], outputs[1], node_grad, edge_grad, grads[0], grads[1], grads[2], grads[3], grads[4], grads[5], grads[6], grads[7], grads[8], grads[9], grads[10], grads[11], grads[12], grads[13], grads[14], grads[15])
```

```python
import functools

import jax
import jax.numpy as jnp
from jax import lax
from jax.experimental import pallas as pl
from jax.experimental.pallas import tpu as pltpu
from jax.sharding import PartitionSpec as P

EPSILON = 1e-05
f32, bf16, i32, i16 = jnp.float32, jnp.bfloat16, jnp.int32, jnp.int16
SMEM = pl.BlockSpec(memory_space=pltpu.SMEM)
VMEM = pl.BlockSpec(memory_space=pltpu.VMEM)
ANY = pl.BlockSpec(memory_space=pl.ANY)
VMEM_BYTES = 60 << 20


def dot(a, b):
    return jnp.dot(a, b, preferred_element_type=f32)


def dot_left(a, b):
    return lax.dot_general(a, b, (((0,), (0,)), ((), ())), preferred_element_type=f32)


def dot_right(a, b):
    return lax.dot_general(a, b, (((1,), (1,)), ((), ())), preferred_element_type=f32)


def row(ref):
    return ref[...].astype(f32)


def silu(x):
    h = 0.5 * x
    return h + h * jnp.tanh(h)


def silu_and_slope(x):
    h = 0.5 * x
    t = jnp.tanh(h)
    s = 0.5 + 0.5 * t
    act = h + h * t
    return act, s + act * (0.5 - 0.5 * t)


def tile_rows(count):
    for rows in (1024, 512, 256, 128):
        if count % rows == 0:
            return rows
    return count


def lane_masks(values, lanes):
    eye = lax.broadcasted_iota(i32, (lanes, lanes), 0) == lax.broadcasted_iota(i32, (lanes, lanes), 1)
    parts = []
    for start in range(0, values[0].shape[1], lanes):
        parts.append(
            jnp.concatenate(
                [jnp.where(eye, v[:, start : start + lanes], 0.0).astype(bf16) for v in values], axis=1
            )
        )
    ones = jnp.ones((lanes, lanes), bf16)
    zeros = jnp.zeros((lanes, lanes), bf16)
    if len(values) == 1:
        spread = ones
    else:
        spread = jnp.concatenate(
            [jnp.concatenate([ones, zeros], 1), jnp.concatenate([zeros, ones], 1)], 0
        )
    return dot(jnp.concatenate(parts, 0), spread)


def chosen_rows(rv, half, rows):
    low = jnp.where(rv >= half, rv - half, rv).astype(i16)
    iota = lax.broadcasted_iota(i32, (half, rows), 0).astype(i16)
    return jnp.where(iota == low, jnp.ones((), bf16), jnp.zeros((), bf16))


def forward_kernel(
    s_ref, r_ref, ext_ref, el_hbm, rv_ref, mk_ref, w1_ref, b1_ref, w2_ref, b2_ref, w3_ref, b3_ref, g_ref, b_ref,
    eo_hbm, p1_hbm, p2_hbm, ce_hbm, sum_ref,
    ts, tr, el, eo, p1, p2, ce, gb, qb, acc, pay, isem, osem,
    *, T, N, NB,
):
    L = el.shape[1]
    H = NB // 2

    def fetch(i):
        d = pl.ds(pl.multiple_of(i * T, T), T)
        return pltpu.make_async_copy(el_hbm.at[d], el.at[d], isem.at[i])

    def flush(i):
        d = pl.ds(pl.multiple_of(i * T, T), T)
        pairs = ((eo, eo_hbm), (p1, p1_hbm), (p2, p2_hbm), (ce, ce_hbm))
        return [pltpu.make_async_copy(v.at[d], h.at[d], osem.at[k, i]) for k, (v, h) in enumerate(pairs)]

    for i in range(N):
        fetch(i).start()
    step = tile_rows(NB)

    def tables(j, _):
        d = pl.ds(pl.multiple_of(j * step, step), step)
        ts[d, :] = dot(ext_ref[d, :], w1_ref[L : 2 * L, :])
        return 0

    def own_table(j, _):
        d = pl.ds(pl.multiple_of(j * step, step), step)
        o = pl.ds(pl.multiple_of(j * step + NB, step), step)
        tr[d, :] = dot(ext_ref[o, :], w1_ref[2 * L :, :]) + row(b1_ref)
        return 0

    lax.fori_loop(0, 3 * NB // step, tables, 0)
    lax.fori_loop(0, NB // step, own_table, 0)

    def gather(i):
        base = pl.multiple_of(i * T, T)
        for e in range(T):
            gb[pl.ds(e, 1), :] = ts[pl.ds(s_ref[base + e], 1), :] + tr[pl.ds(r_ref[base + e], 1), :]

    def scatter(i):
        acc[...] += dot(chosen_rows(rv_ref[i], H, T), pay[...])

    def network(i):
        d = pl.ds(pl.multiple_of(i * T, T), T)
        latent = el[d, :]
        pre1 = dot(latent, w1_ref[:L, :]) + qb[...]
        p1[d, :] = pre1
        pre2 = dot(silu(pre1).astype(bf16), w2_ref[...]) + row(b2_ref)
        p2[d, :] = pre2
        pre3 = dot(silu(pre2).astype(bf16), w3_ref[...]) + row(b3_ref)
        center = pre3 - jnp.mean(pre3, axis=1, keepdims=True)
        ce[d, :] = center
        factor = lax.rsqrt(jnp.mean(center * center, axis=1, keepdims=True) + EPSILON)
        normed = center * factor * row(g_ref) + row(b_ref)
        rv = rv_ref[i]
        masks = lane_masks((mk_ref[i].astype(f32), (rv >= H).astype(f32)), L)
        message = normed * masks[:, :L]
        eo[d, :] = latent.astype(f32) + message
        rounded = message.astype(bf16)
        upper = rounded * masks[:, L:].astype(bf16)
        pay[...] = jnp.concatenate([rounded - upper, upper], axis=1)

    acc[...] = jnp.zeros_like(acc)
    pay[...] = jnp.zeros_like(pay)
    gather(0)
    qb[...] = gb[...]

    def body(i, _):
        fetch(i).wait()
        scatter(jnp.maximum(i - 1, 0))
        gather(jnp.minimum(i + 1, N - 1))
        network(i)
        qb[...] = gb[...]
        for copy in flush(i):
            copy.start()
        return 0

    lax.fori_loop(0, N, body, 0)
    scatter(N - 1)
    sum_ref[:H, :] = acc[:, :L]
    sum_ref[H:, :] = acc[:, L:]

    def finish(i, _):
        for copy in flush(i):
            copy.wait()
        return 0

    lax.fori_loop(0, N, finish, 0)


def edge_forward(s, r, ext, el, mask, weights, NB):
    E, L = el.shape
    T = tile_rows(E)
    N = E // T
    wide = jax.ShapeDtypeStruct((E, L), f32)
    whole = pltpu.VMEM((E, L), f32)
    tile = pltpu.VMEM((T, L), f32)
    return pl.pallas_call(
        functools.partial(forward_kernel, T=T, N=N, NB=NB),
        in_specs=[SMEM, SMEM, VMEM, ANY, VMEM, VMEM] + [VMEM] * 8,
        out_specs=[ANY] * 4 + [VMEM],
        out_shape=[wide] * 4 + [jax.ShapeDtypeStruct((NB, L), f32)],
        scratch_shapes=[
            pltpu.VMEM((3 * NB, L), f32), pltpu.VMEM((NB, L), f32), pltpu.VMEM((E, L), bf16),
            whole, whole, whole, whole, tile, tile,
            pltpu.VMEM((NB // 2, 2 * L), f32), pltpu.VMEM((T, 2 * L), bf16),
            pltpu.SemaphoreType.DMA((N,)), pltpu.SemaphoreType.DMA((4, N)),
        ],
        compiler_params=pltpu.CompilerParams(vmem_limit_bytes=VMEM_BYTES),
        name="edge_forward",
    )(s, r, ext, el, r.reshape(N, 1, T), mask.reshape(N, 1, T), *weights)


def node_kernel(
    sum_ref, nl_ref, pm_ref, nc_ref, w1_ref, b1_ref, w2_ref, b2_ref, w3_ref, b3_ref, g_ref, b_ref,
    no_ref, rg_ref, mg_ref, gw1_ref, gw2_ref, gw3_ref, gv_ref,
    *, T,
):
    NB, L = nl_ref.shape
    gw1_ref[...] = jnp.zeros_like(gw1_ref)
    gw2_ref[...] = jnp.zeros_like(gw2_ref)
    gw3_ref[...] = jnp.zeros_like(gw3_ref)
    gv_ref[...] = jnp.zeros_like(gv_ref)

    def body(i, _):
        d = pl.ds(pl.multiple_of(i * T, T), T)
        latent = nl_ref[d, :]
        inputs = jnp.concatenate([latent, sum_ref[d, :].astype(bf16)], axis=1)
        pre1 = dot(inputs, w1_ref[...]) + row(b1_ref)
        act1, slope1 = silu_and_slope(pre1)
        act1 = act1.astype(bf16)
        pre2 = dot(act1, w2_ref[...]) + row(b2_ref)
        act2, slope2 = silu_and_slope(pre2)
        act2 = act2.astype(bf16)
        pre3 = dot(act2, w3_ref[...]) + row(b3_ref)
        center = pre3 - jnp.mean(pre3, axis=1, keepdims=True)
        factor = lax.rsqrt(jnp.mean(center * center, axis=1, keepdims=True) + EPSILON)
        normed = center * factor
        keep = lane_masks((pm_ref[i].astype(f32),), L)
        no_ref[d, :] = latent.astype(f32) + keep * (normed * row(g_ref) + row(b_ref))
        cot = nc_ref[d, :]
        up = cot * keep
        inner = up * row(g_ref)
        g3 = factor * (
            inner
            - jnp.mean(inner, axis=1, keepdims=True)
            - normed * jnp.mean(inner * normed, axis=1, keepdims=True)
        )
        g3 = g3.astype(bf16)
        g2 = (dot_right(g3, w3_ref[...]) * slope2).astype(bf16)
        g1 = (dot_right(g2, w2_ref[...]) * slope1).astype(bf16)
        gin = dot_right(g1, w1_ref[...])
        rg_ref[d, :] = cot + gin[:, :L]
        mg_ref[d, :] = gin[:, L:]
        gw3_ref[...] += dot_left(act2, g3)
        gw2_ref[...] += dot_left(act1, g2)
        gw1_ref[...] += dot_left(inputs, g1)
        sums = [jnp.sum(v.astype(f32), axis=0, keepdims=True) for v in (g1, g2, g3, up * normed, up)]
        gv_ref[...] += jnp.concatenate(sums + [jnp.zeros((3, L), f32)], axis=0)
        return 0

    lax.fori_loop(0, NB // T, body, 0)


def node_stage(summed, nl, mask, cot, weights):
    NB, L = nl.shape
    T = min(tile_rows(NB), 512)
    rows = jax.ShapeDtypeStruct((NB, L), f32)
    square = jax.ShapeDtypeStruct((L, L), f32)
    return pl.pallas_call(
        functools.partial(node_kernel, T=T),
        in_specs=[VMEM] * 12,
        out_specs=[VMEM] * 7,
        out_shape=[rows, rows, rows, jax.ShapeDtypeStruct((2 * L, L), f32), square, square, jax.ShapeDtypeStruct((8, L), f32)],
        compiler_params=pltpu.CompilerParams(vmem_limit_bytes=VMEM_BYTES),
        name="node_stage",
    )(summed, nl, mask.reshape(NB // T, 1, T), cot, *weights)


def backward_kernel(
    s_ref, r_ref, mg_ref, p1_hbm, p2_hbm, ce_hbm, el_hbm, ct_hbm, rv_ref, mk_ref, w1_ref, w2_ref, w3_ref, g_ref,
    eg_hbm, gs_ref, gr_ref, gw1_ref, gw2_ref, gw3_ref, gv_ref,
    p1, p2, ce, el, ct, gb, qb, g1f, g1c, acc, pay, a0, a1, a2, a3, isem, osem,
    *, T, N, NB,
):
    L = el.shape[1]
    H = NB // 2
    sums = (a0, a1, a2, a3)

    def fetch(i):
        d = pl.ds(pl.multiple_of(i * T, T), T)
        pairs = ((p1, p1_hbm), (p2, p2_hbm), (ce, ce_hbm), (el, el_hbm), (ct, ct_hbm))
        return [pltpu.make_async_copy(h.at[d], v.at[d], isem.at[k, i]) for k, (v, h) in enumerate(pairs)]

    def flush(i):
        d = pl.ds(pl.multiple_of(i * T, T), T)
        return pltpu.make_async_copy(ct.at[d], eg_hbm.at[d], osem.at[i])

    for i in range(N):
        for copy in fetch(i):
            copy.start()
    for ref in (gw1_ref, gw2_ref, gw3_ref, gv_ref, acc, pay, g1c):
        ref[...] = jnp.zeros_like(ref)

    def clear(j, _):
        d = pl.ds(pl.multiple_of(j * 256, 256), 256)
        for a in sums:
            a[d, :] = jnp.zeros((256, L), f32)
        return 0

    lax.fori_loop(0, 3 * NB // 256, clear, 0)

    def gather(i):
        base = pl.multiple_of(i * T, T)
        for e in range(T):
            gb[pl.ds(e, 1), :] = mg_ref[pl.ds(r_ref[base + e], 1), :]

    def scatter(i):
        acc[...] += dot(chosen_rows(rv_ref[i], H, T), pay[...])

    def scatter_senders(i):
        base = pl.multiple_of(i * T, T)
        for e in range(T):
            a = sums[e % len(sums)]
            at = pl.ds(s_ref[base + e], 1)
            a[at, :] += g1c[pl.ds(e, 1), :]

    def network(i):
        d = pl.ds(pl.multiple_of(i * T, T), T)
        center = ce[d, :]
        factor = lax.rsqrt(jnp.mean(center * center, axis=1, keepdims=True) + EPSILON)
        normed = center * factor
        rv = rv_ref[i]
        masks = lane_masks((mk_ref[i].astype(f32), (rv >= H).astype(f32)), L)
        cot = ct[d, :]
        up = (cot + qb[...]) * masks[:, :L]
        inner = up * row(g_ref)
        g3 = factor * (
            inner
            - jnp.mean(inner, axis=1, keepdims=True)
            - normed * jnp.mean(inner * normed, axis=1, keepdims=True)
        )
        g3 = g3.astype(bf16)
        act2, slope2 = silu_and_slope(p2[d, :])
        gw3_ref[...] += dot_left(act2.astype(bf16), g3)
        g2 = (dot_right(g3, w3_ref[...]) * slope2).astype(bf16)
        act1, slope1 = silu_and_slope(p1[d, :])
        gw2_ref[...] += dot_left(act1.astype(bf16), g2)
        g1 = (dot_right(g2, w2_ref[...]) * slope1).astype(bf16)
        gw1_ref[...] += dot_left(el[d, :], g1)
        ct[d, :] = cot + dot_right(g1, w1_ref[:L, :])
        g1f[...] = g1.astype(f32)
        upper = g1 * masks[:, L:].astype(bf16)
        pay[...] = jnp.concatenate([g1 - upper, upper], axis=1)
        cols = [jnp.sum(v.astype(f32), axis=0, keepdims=True) for v in (g1, g2, g3, up * normed, up)]
        gv_ref[...] += jnp.concatenate(cols + [jnp.zeros((3, L), f32)], axis=0)

    gather(0)
    qb[...] = gb[...]

    def body(i, _):
        for copy in fetch(i):
            copy.wait()
        before = jnp.maximum(i - 1, 0)
        scatter(before)
        gather(jnp.minimum(i + 1, N - 1))
        scatter_senders(before)
        network(i)
        qb[...] = gb[...]
        g1c[...] = g1f[...]
        flush(i).start()
        return 0

    lax.fori_loop(0, N, body, 0)
    scatter(N - 1)
    scatter_senders(N - 1)
    gr_ref[:H, :] = acc[:, :L]
    gr_ref[H:, :] = acc[:, L:]

    def merge(j, _):
        d = pl.ds(pl.multiple_of(j * 256, 256), 256)
        gs_ref[d, :] = (a0[d, :] + a1[d, :]) + (a2[d, :] + a3[d, :])
        return 0

    lax.fori_loop(0, 3 * NB // 256, merge, 0)

    def finish(i, _):
        flush(i).wait()
        return 0

    lax.fori_loop(0, N, finish, 0)


def edge_backward(s, r, mg, p1, p2, ce, el, ct, mask, weights, NB):
    E, L = el.shape
    T = tile_rows(E)
    N = E // T
    whole = pltpu.VMEM((E, L), f32)
    tile = pltpu.VMEM((T, L), f32)
    square = jax.ShapeDtypeStruct((L, L), f32)
    return pl.pallas_call(
        functools.partial(backward_kernel, T=T, N=N, NB=NB),
        in_specs=[SMEM, SMEM, VMEM] + [ANY] * 5 + [VMEM] * 6,
        out_specs=[ANY] + [VMEM] * 6,
        out_shape=[
            jax.ShapeDtypeStruct((E, L), f32),
            jax.ShapeDtypeStruct((3 * NB, L), f32), jax.ShapeDtypeStruct((NB, L), f32),
            square, square, square, jax.ShapeDtypeStruct((8, L), f32),
        ],
        scratch_shapes=[
            whole, whole, whole, pltpu.VMEM((E, L), bf16), whole, tile, tile, tile, tile,
            pltpu.VMEM((NB // 2, 2 * L), f32), pltpu.VMEM((T, 2 * L), bf16),
        ]
        + [pltpu.VMEM((3 * NB, L), f32)] * 4
        + [pltpu.SemaphoreType.DMA((5, N)), pltpu.SemaphoreType.DMA((N,))],
        compiler_params=pltpu.CompilerParams(vmem_limit_bytes=VMEM_BYTES),
        name="edge_backward",
    )(s, r, mg, p1, p2, ce, el, ct, r.reshape(N, 1, T), mask.reshape(N, 1, T), *weights)


def with_halo(x):
    count = lax.axis_size("edges")
    up = [(i, i + 1) for i in range(count - 1)]
    down = [(j, i) for i, j in up]
    return jnp.concatenate([lax.ppermute(x, "edges", up), x, lax.ppermute(x, "edges", down)], axis=0)


def passed_along(value, steps):
    count = lax.axis_size("edges")
    first, last = max(0, -steps), min(count, count - steps)
    return lax.ppermute(value, "edges", [(i, i + steps) for i in range(first, last)])


def split_rows(value):
    high = value.astype(bf16)
    return jnp.concatenate([high, (value - high.astype(f32)).astype(bf16)], axis=1)


def shards(
    node_latent, edge_latent, senders, receivers, edge_mask, particle_mask,
    edge_lift, lifting, edge_middle, mixing, edge_final, closing, stretch, offset,
    node_first, opening, node_second, turning, node_third, ending, dilate, displace,
    node_cotangent, edge_cotangent,
):
    NB, L = node_latent.shape
    own = lax.axis_index("edges") * NB
    s = senders - own + NB
    r = receivers - own
    vec = lambda v: v.reshape(1, L)
    ext = with_halo(node_latent)
    eo, p1, p2, ce, partial = edge_forward(
        s, r, ext, edge_latent, edge_mask,
        (edge_lift, vec(lifting), edge_middle, vec(mixing), edge_final, vec(closing), vec(stretch), vec(offset)), NB,
    )
    summed = lax.psum(partial, "rep")
    no, rg, mg, nw1, nw2, nw3, nv = node_stage(
        summed, node_latent, particle_mask, node_cotangent,
        (node_first, vec(opening), node_second, vec(turning), node_third, vec(ending), vec(dilate), vec(displace)),
    )
    share = (lax.axis_index("rep") == 0).astype(f32)
    eg, gs, gr, ew1, ew2, ew3, ev = edge_backward(
        s, r, mg, p1, p2, ce, edge_latent, edge_cotangent, edge_mask,
        (edge_lift, edge_middle, edge_final, vec(stretch)), NB,
    )
    gs2, gr2 = split_rows(gs), split_rows(gr)
    twice = lambda w: jnp.concatenate([w, w], axis=1)
    ext_grad = dot_right(gs2, twice(edge_lift[L : 2 * L]))
    own_grad = dot_right(gr2, twice(edge_lift[2 * L :]))
    fold = lambda w: w[:, :L] + w[:, L:]
    lift = jnp.concatenate([ew1, fold(dot_left(ext, gs2)), fold(dot_left(node_latent, gr2))], axis=0)
    above = passed_along(ext_grad[:NB].astype(bf16), -1).astype(f32)
    below = passed_along(ext_grad[2 * NB :].astype(bf16), 1).astype(f32)
    path = ext_grad[NB : 2 * NB] + own_grad + above + below
    node_grad = rg + lax.psum(path.astype(bf16), "rep").astype(f32)
    t = lax.psum(
        jnp.concatenate([lift, ew2, ew3, ev, share * jnp.concatenate([nw1, nw2, nw3, nv], 0)], axis=0),
        ("edges", "rep"),
    )
    o = 3 * L
    ew2, ew3, ev = t[o : o + L], t[o + L : o + 2 * L], t[o + 2 * L : o + 2 * L + 8]
    o = o + 2 * L + 8
    nw1, nw2, nw3, nv = t[o : o + 2 * L], t[o + 2 * L : o + 3 * L], t[o + 3 * L : o + 4 * L], t[o + 4 * L :]
    return (
        no, eo, node_grad, eg,
        t[: 3 * L], ev[0], ew2, ev[1], ew3, ev[2], ev[3], ev[4],
        nw1, nv[0], nw2, nv[1], nw3, nv[2], nv[3], nv[4],
    )


def solution(mesh):
    node, edge, flat = P("edges", None), P(("edges", "rep"), None), P(("edges", "rep"))
    in_specs = (node, edge, flat, flat, flat, P("edges")) + (P(),) * 16 + (node, edge)
    out_specs = (node, edge, node, edge) + (P(),) * 16
    return jax.shard_map(shards, mesh=mesh, in_specs=in_specs, out_specs=out_specs, check_vma=False)
```

```python
import functools

import jax
import jax.numpy as jnp
from jax import lax
from jax.experimental import pallas as pl
from jax.experimental.pallas import tpu as pltpu
from jax.sharding import PartitionSpec as P

EPSILON = 1e-05
f32, bf16, i32, i16 = jnp.float32, jnp.bfloat16, jnp.int32, jnp.int16
SMEM = pl.BlockSpec(memory_space=pltpu.SMEM)
VMEM = pl.BlockSpec(memory_space=pltpu.VMEM)
ANY = pl.BlockSpec(memory_space=pl.ANY)
VMEM_BYTES = 60 << 20
MESH = pl.DeviceIdType.MESH


def dot(a, b):
    return jnp.dot(a, b, preferred_element_type=f32)


def dot_left(a, b):
    return lax.dot_general(a, b, (((0,), (0,)), ((), ())), preferred_element_type=f32)


def dot_right(a, b):
    return lax.dot_general(a, b, (((1,), (1,)), ((), ())), preferred_element_type=f32)


def row(ref):
    return ref[...].astype(f32)


def silu(x):
    h = 0.5 * x
    return h + h * jnp.tanh(h)


def silu_and_slope(x):
    h = 0.5 * x
    t = jnp.tanh(h)
    s = 0.5 + 0.5 * t
    act = h + h * t
    return act, s + act * (0.5 - 0.5 * t)


def tile_rows(count):
    for rows in (1024, 512, 256, 128):
        if count % rows == 0:
            return rows
    return count


def lane_masks(values, lanes):
    eye = lax.broadcasted_iota(i32, (lanes, lanes), 0) == lax.broadcasted_iota(i32, (lanes, lanes), 1)
    parts = []
    for start in range(0, values[0].shape[1], lanes):
        parts.append(
            jnp.concatenate(
                [jnp.where(eye, v[:, start : start + lanes], 0.0).astype(bf16) for v in values], axis=1
            )
        )
    ones = jnp.ones((lanes, lanes), bf16)
    zeros = jnp.zeros((lanes, lanes), bf16)
    if len(values) == 1:
        spread = ones
    else:
        spread = jnp.concatenate(
            [jnp.concatenate([ones, zeros], 1), jnp.concatenate([zeros, ones], 1)], 0
        )
    return dot(jnp.concatenate(parts, 0), spread)


def chosen_rows(rv, half, rows):
    low = jnp.where(rv >= half, rv - half, rv).astype(i16)
    iota = lax.broadcasted_iota(i32, (half, rows), 0).astype(i16)
    return jnp.where(iota == low, jnp.ones((), bf16), jnp.zeros((), bf16))


def forward_kernel(
    s_ref, r_ref, ext_ref, el_hbm, rv_ref, mk_ref, w1_ref, b1_ref, w2_ref, b2_ref, w3_ref, b3_ref, g_ref, b_ref,
    eo_hbm, p1_hbm, p2_hbm, ce_hbm, sum_ref,
    ts, tr, el, eo, p1, p2, ce, gb, qb, acc, pay, isem, osem,
    *, T, N, NB,
):
    L = el.shape[1]
    H = NB // 2

    def fetch(i):
        d = pl.ds(pl.multiple_of(i * T, T), T)
        return pltpu.make_async_copy(el_hbm.at[d], el.at[d], isem.at[i])

    def flush(i):
        d = pl.ds(pl.multiple_of(i * T, T), T)
        pairs = ((eo, eo_hbm), (p1, p1_hbm), (p2, p2_hbm), (ce, ce_hbm))
        return [pltpu.make_async_copy(v.at[d], h.at[d], osem.at[k, i]) for k, (v, h) in enumerate(pairs)]

    for i in range(N):
        fetch(i).start()
    step = tile_rows(NB)

    def tables(j, _):
        d = pl.ds(pl.multiple_of(j * step, step), step)
        ts[d, :] = dot(ext_ref[d, :], w1_ref[L : 2 * L, :])
        return 0

    def own_table(j, _):
        d = pl.ds(pl.multiple_of(j * step, step), step)
        o = pl.ds(pl.multiple_of(j * step + NB, step), step)
        tr[d, :] = dot(ext_ref[o, :], w1_ref[2 * L :, :]) + row(b1_ref)
        return 0

    lax.fori_loop(0, 3 * NB // step, tables, 0)
    lax.fori_loop(0, NB // step, own_table, 0)

    def gather(i):
        base = pl.multiple_of(i * T, T)
        for e in range(T):
            gb[pl.ds(e, 1), :] = ts[pl.ds(s_ref[base + e], 1), :] + tr[pl.ds(r_ref[base + e], 1), :]

    def scatter(i):
        acc[...] += dot(chosen_rows(rv_ref[i], H, T), pay[...])

    def network(i):
        d = pl.ds(pl.multiple_of(i * T, T), T)
        latent = el[d, :]
        pre1 = dot(latent, w1_ref[:L, :]) + qb[...]
        p1[d, :] = pre1
        pre2 = dot(silu(pre1).astype(bf16), w2_ref[...]) + row(b2_ref)
        p2[d, :] = pre2
        pre3 = dot(silu(pre2).astype(bf16), w3_ref[...]) + row(b3_ref)
        center = pre3 - jnp.mean(pre3, axis=1, keepdims=True)
        ce[d, :] = center
        factor = lax.rsqrt(jnp.mean(center * center, axis=1, keepdims=True) + EPSILON)
        normed = center * factor * row(g_ref) + row(b_ref)
        rv = rv_ref[i]
        masks = lane_masks((mk_ref[i].astype(f32), (rv >= H).astype(f32)), L)
        message = normed * masks[:, :L]
        eo[d, :] = latent.astype(f32) + message
        rounded = message.astype(bf16)
        upper = rounded * masks[:, L:].astype(bf16)
        pay[...] = jnp.concatenate([rounded - upper, upper], axis=1)

    acc[...] = jnp.zeros_like(acc)
    pay[...] = jnp.zeros_like(pay)
    gather(0)
    qb[...] = gb[...]

    def body(i, _):
        fetch(i).wait()
        scatter(jnp.maximum(i - 1, 0))
        gather(jnp.minimum(i + 1, N - 1))
        network(i)
        qb[...] = gb[...]
        for copy in flush(i):
            copy.start()
        return 0

    lax.fori_loop(0, N, body, 0)
    scatter(N - 1)
    sum_ref[:H, :] = acc[:, :L]
    sum_ref[H:, :] = acc[:, L:]

    def finish(i, _):
        for copy in flush(i):
            copy.wait()
        return 0

    lax.fori_loop(0, N, finish, 0)


def edge_forward(s, r, ext, el, mask, weights, NB):
    E, L = el.shape
    T = tile_rows(E)
    N = E // T
    wide = jax.ShapeDtypeStruct((E, L), f32)
    whole = pltpu.VMEM((E, L), f32)
    tile = pltpu.VMEM((T, L), f32)
    return pl.pallas_call(
        functools.partial(forward_kernel, T=T, N=N, NB=NB),
        in_specs=[SMEM, SMEM, VMEM, ANY, VMEM, VMEM] + [VMEM] * 8,
        out_specs=[ANY] * 4 + [VMEM],
        out_shape=[wide] * 4 + [jax.ShapeDtypeStruct((NB, L), f32)],
        scratch_shapes=[
            pltpu.VMEM((3 * NB, L), f32), pltpu.VMEM((NB, L), f32), pltpu.VMEM((E, L), bf16),
            whole, whole, whole, whole, tile, tile,
            pltpu.VMEM((NB // 2, 2 * L), f32), pltpu.VMEM((T, 2 * L), bf16),
            pltpu.SemaphoreType.DMA((N,)), pltpu.SemaphoreType.DMA((4, N)),
        ],
        compiler_params=pltpu.CompilerParams(vmem_limit_bytes=VMEM_BYTES),
        name="edge_forward",
    )(s, r, ext, el, r.reshape(N, 1, T), mask.reshape(N, 1, T), *weights)


def remote(src, dst, send, recv, device):
    return pltpu.make_async_remote_copy(
        src_ref=src, dst_ref=dst, send_sem=send, recv_sem=recv, device_id=device, device_id_type=MESH
    )


def halo_kernel(nl_ref, s_ref, r_ref, ext_ref, sl_ref, rl_ref, send, recv, *, n, K):
    NB, L = nl_ref.shape
    H = NB // 2
    C = H // K
    e, r = lax.axis_index("edges"), lax.axis_index("rep")
    h = r % 2
    peer, below, above = (e, r + 1 - 2 * h), (e - 1, r), (e + 1, r)
    has_below, has_above = e > 0, e < n - 1
    barrier = pltpu.get_barrier_semaphore()
    pl.semaphore_signal(barrier, inc=1, device_id=peer, device_id_type=MESH)

    @pl.when(has_below)
    def _():
        pl.semaphore_signal(barrier, inc=1, device_id=below, device_id_type=MESH)

    @pl.when(has_above)
    def _():
        pl.semaphore_signal(barrier, inc=1, device_id=above, device_id_type=MESH)

    pl.semaphore_wait(barrier, 1 + has_below.astype(i32) + has_above.astype(i32))

    def rows(start, c):
        return pl.ds(pl.multiple_of(start + h * H + c * C, 16), C)

    def to_above(c):
        return remote(nl_ref.at[rows(0, c)], ext_ref.at[rows(0, c)], send.at[0, c], recv.at[0, c], above)

    def to_below(c):
        return remote(nl_ref.at[rows(0, c)], ext_ref.at[rows(2 * NB, c)], send.at[1, c], recv.at[1, c], below)

    def pass_first(c):
        d = rows(0, c)
        return remote(ext_ref.at[d], ext_ref.at[d], send.at[2, c], recv.at[2, c], peer)

    def pass_last(c):
        d = rows(2 * NB, c)
        return remote(ext_ref.at[d], ext_ref.at[d], send.at[3, c], recv.at[3, c], peer)

    for c in range(K):

        @pl.when(has_above)
        def _():
            to_above(c).start()

        @pl.when(has_below)
        def _():
            to_below(c).start()

    ext_ref[NB : 2 * NB, :] = nl_ref[...]
    sl_ref[...] = s_ref[...] - (e - 1) * NB
    rl_ref[...] = r_ref[...] - e * NB

    @pl.when(jnp.logical_not(has_below))
    def _():
        ext_ref[:NB, :] = jnp.zeros((NB, L), ext_ref.dtype)

    @pl.when(jnp.logical_not(has_above))
    def _():
        ext_ref[2 * NB :, :] = jnp.zeros((NB, L), ext_ref.dtype)

    for c in range(K):

        @pl.when(has_below)
        def _():
            to_above(c).wait_recv()
            pass_first(c).start()

        @pl.when(has_above)
        def _():
            to_below(c).wait_recv()
            pass_last(c).start()

    for c in range(K):

        @pl.when(has_below)
        def _():
            pass_first(c).wait()
            to_below(c).wait_send()

        @pl.when(has_above)
        def _():
            pass_last(c).wait()
            to_above(c).wait_send()


def halo_stage(nl, s, r, n):
    NB, L = nl.shape
    flat = jax.ShapeDtypeStruct(s.shape, i32)
    return pl.pallas_call(
        functools.partial(halo_kernel, n=n, K=4),
        in_specs=[VMEM] * 3,
        out_specs=[VMEM] * 3,
        out_shape=[jax.ShapeDtypeStruct((3 * NB, L), nl.dtype), flat, flat],
        scratch_shapes=[pltpu.SemaphoreType.DMA((4, 4)), pltpu.SemaphoreType.DMA((4, 4))],
        compiler_params=pltpu.CompilerParams(vmem_limit_bytes=VMEM_BYTES, collective_id=0, has_side_effects=True),
        name="halo",
    )(nl, s, r)


def node_kernel(
    part_ref, nl_ref, pm_ref, nc_ref, w1_ref, b1_ref, w2_ref, b2_ref, w3_ref, b3_ref, g_ref, b_ref,
    no_ref, rg_ref, mg_ref, gw1_ref, gw2_ref, gw3_ref, gv_ref,
    rbuf, xs, xr, sm, send, recv,
    *, K,
):
    NB, L = nl_ref.shape
    H = NB // 2
    C = H // K
    e, r = lax.axis_index("edges"), lax.axis_index("rep")
    h, x = r % 2, r // 2
    peer, across = (e, r + 1 - 2 * h), (e, (r + 2) % 4)
    barrier = pltpu.get_barrier_semaphore()
    for device in (peer, across):
        pl.semaphore_signal(barrier, inc=1, device_id=device, device_id_type=MESH)
    pl.semaphore_wait(barrier, 2)

    def at(half, c):
        return pl.ds(pl.multiple_of(half * H + c * C, C), C)

    def halves(c):
        return remote(part_ref.at[at(1 - h, c)], rbuf.at[pl.ds(c * C, C)], send.at[0, c], recv.at[0, c], peer)

    def exchange(c):
        d = pl.ds(pl.multiple_of(c * C, C), C)
        return remote(xs.at[d], xr.at[d], send.at[1, c], recv.at[1, c], across)

    def share(c):
        d = at(h, c)
        return remote(sm.at[d], sm.at[d], send.at[2, c], recv.at[2, c], peer)

    def arrived(c):
        d = at(1 - h, c)
        return remote(sm.at[d], sm.at[d], send.at[2, c], recv.at[2, c], peer)

    for c in range(K):
        halves(c).start()
    for c in range(K):
        halves(c).wait_recv()
        d = pl.ds(c * C, C)
        xs[d, :] = part_ref[at(h, c), :] + rbuf[d, :]
        exchange(c).start()
    for ref in (gw1_ref, gw2_ref, gw3_ref, gv_ref):
        ref[...] = jnp.zeros_like(ref)

    def body(q, _):
        c, mine = q // 2, q % 2 == 0
        half = jnp.where(mine, h, 1 - h)
        d = at(half, c)

        @pl.when(mine)
        def _():
            exchange(c).wait_recv()
            o = pl.ds(pl.multiple_of(c * C, C), C)
            sm[d, :] = (xs[o, :] + xr[o, :]).astype(bf16)
            share(c).start()

        @pl.when(jnp.logical_not(mine))
        def _():
            arrived(c).wait_recv()

        latent = nl_ref[d, :]
        inputs = jnp.concatenate([latent, sm[d, :]], axis=1)
        pre1 = dot(inputs, w1_ref[...]) + row(b1_ref)
        act1, slope1 = silu_and_slope(pre1)
        act1 = act1.astype(bf16)
        pre2 = dot(act1, w2_ref[...]) + row(b2_ref)
        act2, slope2 = silu_and_slope(pre2)
        act2 = act2.astype(bf16)
        pre3 = dot(act2, w3_ref[...]) + row(b3_ref)
        center = pre3 - jnp.mean(pre3, axis=1, keepdims=True)
        factor = lax.rsqrt(jnp.mean(center * center, axis=1, keepdims=True) + EPSILON)
        normed = center * factor
        keep = lane_masks((pm_ref[half * K + c].astype(f32),), L)
        no_ref[d, :] = latent.astype(f32) + keep * (normed * row(g_ref) + row(b_ref))
        cot = nc_ref[d, :]
        up = cot * keep
        inner = up * row(g_ref)
        g3 = factor * (
            inner
            - jnp.mean(inner, axis=1, keepdims=True)
            - normed * jnp.mean(inner * normed, axis=1, keepdims=True)
        )
        g3 = g3.astype(bf16)
        g2 = (dot_right(g3, w3_ref[...]) * slope2).astype(bf16)
        g1 = (dot_right(g2, w2_ref[...]) * slope1).astype(bf16)
        gin = dot_right(g1, w1_ref[...])
        rg_ref[d, :] = cot + gin[:, :L]
        mg_ref[d, :] = gin[:, L:]

        @pl.when(jnp.logical_and(mine, c * 2 // K == x))
        def _():
            gw3_ref[...] += dot_left(act2, g3)
            gw2_ref[...] += dot_left(act1, g2)
            gw1_ref[...] += dot_left(inputs, g1)
            sums = [jnp.sum(v.astype(f32), axis=0, keepdims=True) for v in (g1, g2, g3, up * normed, up)]
            gv_ref[...] += jnp.concatenate(sums + [jnp.zeros((3, L), f32)], axis=0)

        return 0

    lax.fori_loop(0, 2 * K, body, 0)
    for c in range(K):
        halves(c).wait_send()
        exchange(c).wait_send()
        share(c).wait_send()


def node_stage(partial, nl, mask, cot, weights):
    NB, L = nl.shape
    K = 2
    H = NB // 2
    rows = jax.ShapeDtypeStruct((NB, L), f32)
    square = jax.ShapeDtypeStruct((L, L), f32)
    return pl.pallas_call(
        functools.partial(node_kernel, K=K),
        in_specs=[VMEM] * 12,
        out_specs=[VMEM] * 7,
        out_shape=[rows, rows, rows, jax.ShapeDtypeStruct((2 * L, L), f32), square, square, jax.ShapeDtypeStruct((8, L), f32)],
        scratch_shapes=[
            pltpu.VMEM((H, L), f32), pltpu.VMEM((H, L), f32), pltpu.VMEM((H, L), f32), pltpu.VMEM((NB, L), bf16),
            pltpu.SemaphoreType.DMA((3, K)), pltpu.SemaphoreType.DMA((3, K)),
        ],
        compiler_params=pltpu.CompilerParams(vmem_limit_bytes=VMEM_BYTES, collective_id=1, has_side_effects=True),
        name="node_stage",
    )(partial, nl, mask.reshape(2 * K, 1, H // K), cot, *weights)


def backward_kernel(
    s_ref, r_ref, mg_ref, p1_hbm, p2_hbm, ce_hbm, el_hbm, ct_hbm, ni_hbm, rv_ref, mk_ref, w1_ref, w2_ref, w3_ref, g_ref,
    eg_hbm, no_hbm, gs_ref, gr_ref, gw1_ref, gw2_ref, gw3_ref, gv_ref,
    p1, p2, ce, el, ct, gb, qb, g1f, g1c, acc, pay, a0, a1, a2, a3, isem, osem, nsem,
    *, T, N, NB,
):
    L = el.shape[1]
    H = NB // 2
    sums = (a0, a1, a2, a3)

    def fetch(i):
        d = pl.ds(pl.multiple_of(i * T, T), T)
        pairs = ((p1, p1_hbm), (p2, p2_hbm), (ce, ce_hbm), (el, el_hbm), (ct, ct_hbm))
        return [pltpu.make_async_copy(h.at[d], v.at[d], isem.at[k, i]) for k, (v, h) in enumerate(pairs)]

    def flush(i):
        d = pl.ds(pl.multiple_of(i * T, T), T)
        return pltpu.make_async_copy(ct.at[d], eg_hbm.at[d], osem.at[i])

    for i in range(N):
        for copy in fetch(i):
            copy.start()
    through = pltpu.make_async_copy(ni_hbm, no_hbm, nsem)
    through.start()
    for ref in (gw1_ref, gw2_ref, gw3_ref, gv_ref, acc, pay, g1c):
        ref[...] = jnp.zeros_like(ref)

    def clear(j, _):
        d = pl.ds(pl.multiple_of(j * 256, 256), 256)
        for a in sums:
            a[d, :] = jnp.zeros((256, L), f32)
        return 0

    lax.fori_loop(0, 3 * NB // 256, clear, 0)

    def gather(i):
        base = pl.multiple_of(i * T, T)
        for e in range(T):
            gb[pl.ds(e, 1), :] = mg_ref[pl.ds(r_ref[base + e], 1), :]

    def scatter(i):
        acc[...] += dot(chosen_rows(rv_ref[i], H, T), pay[...])

    def scatter_senders(i):
        base = pl.multiple_of(i * T, T)
        for e in range(T):
            a = sums[e % len(sums)]
            at = pl.ds(s_ref[base + e], 1)
            a[at, :] += g1c[pl.ds(e, 1), :]

    def network(i):
        d = pl.ds(pl.multiple_of(i * T, T), T)
        center = ce[d, :]
        factor = lax.rsqrt(jnp.mean(center * center, axis=1, keepdims=True) + EPSILON)
        normed = center * factor
        rv = rv_ref[i]
        masks = lane_masks((mk_ref[i].astype(f32), (rv >= H).astype(f32)), L)
        cot = ct[d, :]
        up = (cot + qb[...]) * masks[:, :L]
        inner = up * row(g_ref)
        g3 = factor * (
            inner
            - jnp.mean(inner, axis=1, keepdims=True)
            - normed * jnp.mean(inner * normed, axis=1, keepdims=True)
        )
        g3 = g3.astype(bf16)
        act2, slope2 = silu_and_slope(p2[d, :])
        gw3_ref[...] += dot_left(act2.astype(bf16), g3)
        g2 = (dot_right(g3, w3_ref[...]) * slope2).astype(bf16)
        act1, slope1 = silu_and_slope(p1[d, :])
        gw2_ref[...] += dot_left(act1.astype(bf16), g2)
        g1 = (dot_right(g2, w2_ref[...]) * slope1).astype(bf16)
        gw1_ref[...] += dot_left(el[d, :], g1)
        ct[d, :] = cot + dot_right(g1, w1_ref[:L, :])
        g1f[...] = g1.astype(f32)
        upper = g1 * masks[:, L:].astype(bf16)
        pay[...] = jnp.concatenate([g1 - upper, upper], axis=1)
        cols = [jnp.sum(v.astype(f32), axis=0, keepdims=True) for v in (g1, g2, g3, up * normed, up)]
        gv_ref[...] += jnp.concatenate(cols + [jnp.zeros((3, L), f32)], axis=0)

    gather(0)
    qb[...] = gb[...]

    def body(i, _):
        for copy in fetch(i):
            copy.wait()
        before = jnp.maximum(i - 1, 0)
        scatter(before)
        gather(jnp.minimum(i + 1, N - 1))
        scatter_senders(before)
        network(i)
        qb[...] = gb[...]
        g1c[...] = g1f[...]
        flush(i).start()
        return 0

    lax.fori_loop(0, N, body, 0)
    scatter(N - 1)
    scatter_senders(N - 1)
    gr_ref[:H, :] = acc[:, :L]
    gr_ref[H:, :] = acc[:, L:]

    def merge(j, _):
        d = pl.ds(pl.multiple_of(j * 256, 256), 256)
        gs_ref[d, :] = (a0[d, :] + a1[d, :]) + (a2[d, :] + a3[d, :])
        return 0

    lax.fori_loop(0, 3 * NB // 256, merge, 0)

    def finish(i, _):
        flush(i).wait()
        return 0

    lax.fori_loop(0, N, finish, 0)
    through.wait()


def edge_backward(s, r, mg, p1, p2, ce, el, ct, no, mask, weights, NB):
    E, L = el.shape
    T = tile_rows(E)
    N = E // T
    whole = pltpu.VMEM((E, L), f32)
    tile = pltpu.VMEM((T, L), f32)
    square = jax.ShapeDtypeStruct((L, L), f32)
    return pl.pallas_call(
        functools.partial(backward_kernel, T=T, N=N, NB=NB),
        in_specs=[SMEM, SMEM, VMEM] + [ANY] * 6 + [VMEM] * 6,
        out_specs=[ANY] * 2 + [VMEM] * 6,
        out_shape=[
            jax.ShapeDtypeStruct((E, L), f32), jax.ShapeDtypeStruct((NB, L), f32),
            jax.ShapeDtypeStruct((3 * NB, L), f32), jax.ShapeDtypeStruct((NB, L), f32),
            square, square, square, jax.ShapeDtypeStruct((8, L), f32),
        ],
        scratch_shapes=[
            whole, whole, whole, pltpu.VMEM((E, L), bf16), whole, tile, tile, tile, tile,
            pltpu.VMEM((NB // 2, 2 * L), f32), pltpu.VMEM((T, 2 * L), bf16),
        ]
        + [pltpu.VMEM((3 * NB, L), f32)] * 4
        + [pltpu.SemaphoreType.DMA((5, N)), pltpu.SemaphoreType.DMA((N,)), pltpu.SemaphoreType.DMA],
        compiler_params=pltpu.CompilerParams(vmem_limit_bytes=VMEM_BYTES),
        name="edge_backward",
    )(s, r, mg, p1, p2, ce, el, ct, no, r.reshape(N, 1, T), mask.reshape(N, 1, T), *weights)


def split_rows(value):
    high = value.astype(bf16)
    return jnp.concatenate([high, (value - high.astype(f32)).astype(bf16)], axis=1)


def tail_kernel(
    gs_ref, gr_ref, ext_ref, w1_ref, ew1_ref, ew2_ref, ew3_ref, ev_ref, nw1_ref, nw2_ref, nw3_ref, nv_ref,
    tot, pt_ref,
    hs, hr, hk, ys, yr, ob, obr, xs, xr, pb, pr, ps, prs, ag, agf, send, recv, gsend, grecv, asend, arecv,
    *, n, K, R,
):
    L = gr_ref.shape[1]
    NB = gr_ref.shape[0]
    H = NB // 2
    C = H // K
    G = 2 * n
    PH = G * R
    e, r = lax.axis_index("edges"), lax.axis_index("rep")
    h, x = r % 2, r // 2
    me = x * n + e
    peer, across, below, above = (e, r + 1 - 2 * h), (e, (r + 2) % 4), (e - 1, r), (e + 1, r)
    has_below, has_above = e > 0, e < n - 1

    def member(k):
        j = (me + k) % G
        return j, (j % n, (j // n) * 2 + h)

    barrier = pltpu.get_barrier_semaphore()
    pl.semaphore_signal(barrier, inc=1, device_id=peer, device_id_type=MESH)

    def greet(k, _):
        pl.semaphore_signal(barrier, inc=1, device_id=member(k)[1], device_id_type=MESH)
        return 0

    lax.fori_loop(1, G, greet, 0)

    def twice(w):
        return jnp.concatenate([w, w], axis=1)

    ws = twice(w1_ref[L : 2 * L, :])
    wr = twice(w1_ref[2 * L :, :])

    def at(half, c):
        return pl.ds(pl.multiple_of(half * H + c * C, C), C)

    def block(start, half, c):
        return dot_right(split_rows(gs_ref[pl.ds(pl.multiple_of(start + half * H + c * C, C), C), :]), ws)

    def own_block(half, c):
        return block(NB, half, c) + dot_right(split_rows(gr_ref[at(half, c), :]), wr)

    def pair_copy(k, c):
        return remote(hs.at[k, pl.ds(c * C, C)], hr.at[k, pl.ds(c * C, C)], send.at[k, c], recv.at[k, c], peer)

    def neighbour_copy(k, c):
        d = pl.ds(c * C, C)
        return remote(ys.at[k, d], yr.at[k, d], send.at[2 + k, c], recv.at[2 + k, c], below if k == 0 else above)

    def own_copy(c):
        d = pl.ds(c * C, C)
        return remote(ob.at[d], obr.at[d], send.at[4, c], recv.at[4, c], peer)

    def across_copy(c):
        d = pl.ds(c * C, C)
        return remote(xs.at[d], xr.at[d], send.at[5, c], recv.at[5, c], across)

    def total_copy(c):
        d = at(h, c)
        return remote(tot.at[d], tot.at[d], send.at[6, c], recv.at[6, c], peer)

    def total_arrived(c):
        d = at(1 - h, c)
        return remote(tot.at[d], tot.at[d], send.at[6, c], recv.at[6, c], peer)

    for c in range(K):
        for k in (0, 1):
            hs[k, pl.ds(c * C, C), :] = block(2 * NB * k, 1 - h, c).astype(bf16)
        if c == 0:
            pl.semaphore_wait(barrier, G)
        for k in (0, 1):
            pair_copy(k, c).start()
    for c in range(K):
        for k in (0, 1):
            hk[k, pl.ds(c * C, C), :] = block(2 * NB * k, h, c)
    for c in range(K):
        d = pl.ds(c * C, C)
        for k in (0, 1):
            pair_copy(k, c).wait_recv()
            ys[k, d, :] = (hk[k, d, :] + hr[k, d, :].astype(f32)).astype(bf16)

        @pl.when(has_below)
        def _():
            neighbour_copy(0, c).start()

        @pl.when(has_above)
        def _():
            neighbour_copy(1, c).start()

    pb[...] = jnp.zeros_like(pb)
    pb[:L, :] = ew1_ref[...]

    def lift(j, total):
        d = pl.ds(pl.multiple_of(j * C, C), C)
        return total + dot_left(ext_ref[d, :], split_rows(gs_ref[d, :]))

    def lift_own(j, total):
        d = pl.ds(pl.multiple_of(j * C, C), C)
        o = pl.ds(pl.multiple_of(NB + j * C, C), C)
        return total + dot_left(ext_ref[o, :], split_rows(gr_ref[d, :]))

    t = lax.fori_loop(0, 3 * NB // C, lift, jnp.zeros((L, 2 * L), f32))
    pb[L : 2 * L, :] = t[:, :L] + t[:, L:]
    t = lax.fori_loop(0, NB // C, lift_own, jnp.zeros((L, 2 * L), f32))
    pb[2 * L : 3 * L, :] = t[:, :L] + t[:, L:]
    o = 3 * L
    for ref in (ew2_ref, ew3_ref, ev_ref, nw1_ref, nw2_ref, nw3_ref, nv_ref):
        pb[o : o + ref.shape[0], :] = ref[...]
        o += ref.shape[0]

    def params_half(half):
        return pl.ds(pl.multiple_of(half * PH, 16), PH)

    params_pair = remote(pb.at[params_half(1 - h)], pr, asend.at[0], arecv.at[0], peer)
    params_pair.start()
    for c in range(K):
        ob[pl.ds(c * C, C), :] = own_block(1 - h, c)
        own_copy(c).start()
    params_pair.wait_recv()
    ps[...] = (pb[params_half(h), :] + pr[...]).astype(bf16)

    def share_rows(j):
        return pl.ds(pl.multiple_of(j * R, 16), R)

    def spread(k):
        j, device = member(k)
        return remote(ps.at[share_rows(j)], prs.at[share_rows(me)], gsend.at[0, k], grecv.at[0, me], device)

    def spread_arrived(k):
        j, device = member(k)
        return remote(ps.at[share_rows(j)], prs.at[share_rows(j)], gsend.at[0, k], grecv.at[0, j], device)

    def collect(k):
        j, device = member(k)
        return remote(ag.at[share_rows(me)], ag.at[share_rows(me)], gsend.at[1, k], grecv.at[1, me], device)

    def collect_arrived(k):
        j, device = member(k)
        return remote(ag.at[share_rows(j)], ag.at[share_rows(j)], gsend.at[1, k], grecv.at[1, j], device)

    def start_spread(k, _):
        spread(k).start()
        return 0

    lax.fori_loop(1, G, start_spread, 0)

    def path(c):
        d = pl.ds(c * C, C)
        own_copy(c).wait_recv()
        tot[at(h, c), :] = own_block(h, c) + obr[d, :]

    def neighbours(c):
        d = pl.ds(c * C, C)

        @pl.when(has_above)
        def _():
            neighbour_copy(0, c).wait_recv()
            tot[at(h, c), :] += yr[0, d, :].astype(f32)

        @pl.when(has_below)
        def _():
            neighbour_copy(1, c).wait_recv()
            tot[at(h, c), :] += yr[1, d, :].astype(f32)

        xs[d, :] = tot[at(h, c), :].astype(bf16)
        across_copy(c).start()

    def finish(c):
        d = pl.ds(c * C, C)
        across_copy(c).wait_recv()
        tot[at(h, c), :] = xs[d, :].astype(f32) + xr[d, :].astype(f32)
        total_copy(c).start()

    for c in range(K):
        path(c)
    for c in range(K // 2):
        neighbours(c)

    def add_share(k, total):
        spread_arrived(k).wait_recv()
        return total + prs[share_rows(member(k)[0]), :].astype(f32)

    ag[share_rows(me), :] = lax.fori_loop(1, G, add_share, ps[share_rows(me), :].astype(f32)).astype(bf16)

    def start_collect(k, _):
        collect(k).start()
        return 0

    lax.fori_loop(1, G, start_collect, 0)
    for c in range(K // 2, K):
        neighbours(c)
    for c in range(K):
        finish(c)

    def end_collect(k, _):
        collect_arrived(k).wait_recv()
        return 0

    lax.fori_loop(1, G, end_collect, 0)
    params_all = remote(ag, agf, asend.at[1], arecv.at[1], peer)
    params_all.start()
    pt_ref[params_half(h), :] = ag[...].astype(f32)
    for c in range(K):
        total_arrived(c).wait_recv()
    params_all.wait_recv()
    pt_ref[params_half(1 - h), :] = agf[...].astype(f32)

    def end_sends(k, _):
        spread(k).wait_send()
        collect(k).wait_send()
        return 0

    lax.fori_loop(1, G, end_sends, 0)
    params_pair.wait_send()
    params_all.wait_send()
    for c in range(K):
        pair_copy(0, c).wait_send()
        pair_copy(1, c).wait_send()
        own_copy(c).wait_send()
        across_copy(c).wait_send()
        total_copy(c).wait_send()

        @pl.when(has_below)
        def _():
            neighbour_copy(0, c).wait_send()

        @pl.when(has_above)
        def _():
            neighbour_copy(1, c).wait_send()


def tail_stage(gs, gr, ext, w1, parts, n):
    NB, L = gr.shape
    H, K, G = NB // 2, 4, 2 * n
    count = 2 * L + sum(p.shape[0] for p in parts)
    R = -(-count // (2 * G * 16)) * 16
    PH = G * R
    half = lambda kind: pltpu.VMEM((H, L), kind)
    two = lambda kind: pltpu.VMEM((2, H, L), kind)
    par = lambda kind: pltpu.VMEM((PH, L), kind)
    sem = pltpu.SemaphoreType.DMA
    return pl.pallas_call(
        functools.partial(tail_kernel, n=n, K=K, R=R),
        in_specs=[VMEM] * (4 + len(parts)),
        out_specs=[VMEM] * 2,
        out_shape=[jax.ShapeDtypeStruct((NB, L), f32), jax.ShapeDtypeStruct((2 * PH, L), f32)],
        scratch_shapes=[
            two(bf16), two(bf16), two(f32), two(bf16), two(bf16), half(f32), half(f32), half(bf16), half(bf16),
            pltpu.VMEM((2 * PH, L), f32), par(f32), par(bf16), par(bf16), par(bf16), par(bf16),
            sem((7, K)), sem((7, K)), sem((2, G)), sem((2, G)), sem((2,)), sem((2,)),
        ],
        compiler_params=pltpu.CompilerParams(vmem_limit_bytes=VMEM_BYTES, collective_id=2, has_side_effects=True),
        name="tail",
    )(gs, gr, ext, w1, *parts)


def finish_kernel(tot_ref, rg_ref, pt_ref, ng_ref, *outs):
    ng_ref[...] = rg_ref[...] + tot_ref[...]
    L = tot_ref.shape[1]
    first, after = 3 * L + 2 * L, 3 * L + 2 * L + 8
    second = after + 4 * L
    spots = [
        (0, 3 * L), first, (3 * L, L), first + 1, (4 * L, L), first + 2, first + 3, first + 4,
        (after, 2 * L), second, (after + 2 * L, L), second + 1, (after + 3 * L, L), second + 2, second + 3, second + 4,
    ]
    for out, spot in zip(outs, spots):
        if isinstance(spot, tuple):
            out[...] = pt_ref[spot[0] : spot[0] + spot[1], :]
        else:
            out[...] = pt_ref[spot, :]


def finish_stage(tot, rg, pt):
    L = tot.shape[1]
    mat = lambda k: jax.ShapeDtypeStruct((k * L, L), f32)
    vec = jax.ShapeDtypeStruct((L,), f32)
    shapes = [mat(3), vec, mat(1), vec, mat(1), vec, vec, vec, mat(2), vec, mat(1), vec, mat(1), vec, vec, vec]
    return pl.pallas_call(
        finish_kernel,
        in_specs=[VMEM] * 3,
        out_specs=[VMEM] * 17,
        out_shape=[jax.ShapeDtypeStruct(tot.shape, f32)] + shapes,
        compiler_params=pltpu.CompilerParams(vmem_limit_bytes=VMEM_BYTES),
        name="finish",
    )(tot, rg, pt)


def shards(
    node_latent, edge_latent, senders, receivers, edge_mask, particle_mask,
    edge_lift, lifting, edge_middle, mixing, edge_final, closing, stretch, offset,
    node_first, opening, node_second, turning, node_third, ending, dilate, displace,
    node_cotangent, edge_cotangent,
):
    NB, L = node_latent.shape
    vec = lambda v: v.reshape(1, L)
    n = lax.axis_size("edges")
    ext, s, r = halo_stage(node_latent, senders, receivers, n)
    eo, p1, p2, ce, partial = edge_forward(
        s, r, ext, edge_latent, edge_mask,
        (edge_lift, vec(lifting), edge_middle, vec(mixing), edge_final, vec(closing), vec(stretch), vec(offset)), NB,
    )
    no, rg, mg, nw1, nw2, nw3, nv = node_stage(
        partial, node_latent, particle_mask, node_cotangent,
        (node_first, vec(opening), node_second, vec(turning), node_third, vec(ending), vec(dilate), vec(displace)),
    )
    eg, no, gs, gr, ew1, ew2, ew3, ev = edge_backward(
        s, r, mg, p1, p2, ce, edge_latent, edge_cotangent, no, edge_mask,
        (edge_lift, edge_middle, edge_final, vec(stretch)), NB,
    )
    path, totals = tail_stage(gs, gr, ext, edge_lift, (ew1, ew2, ew3, ev, nw1, nw2, nw3, nv), n)
    node_grad, *grads = finish_stage(path, rg, totals)
    return (no, eo, node_grad, eg, *grads)


def solution(mesh):
    node, edge, flat = P("edges", None), P(("edges", "rep"), None), P(("edges", "rep"))
    in_specs = (node, edge, flat, flat, flat, P("edges")) + (P(),) * 16 + (node, edge)
    out_specs = (node, edge, node, edge) + (P(),) * 16
    return jax.shard_map(shards, mesh=mesh, in_specs=in_specs, out_specs=out_specs, check_vma=False)
```

```python
import functools

import jax
import jax.numpy as jnp
from jax import lax
from jax.experimental import pallas as pl
from jax.experimental.pallas import tpu as pltpu
from jax.sharding import PartitionSpec as P

EPSILON = 1e-05
f32, bf16, i32, i16 = jnp.float32, jnp.bfloat16, jnp.int32, jnp.int16
SMEM = pl.BlockSpec(memory_space=pltpu.SMEM)
VMEM = pl.BlockSpec(memory_space=pltpu.VMEM)
ANY = pl.BlockSpec(memory_space=pl.ANY)
VMEM_BYTES = 62 << 20
ACCUMULATORS = 4
LANES = 128
MESH = pl.DeviceIdType.MESH


def dot(a, b):
    return jnp.dot(a, b, preferred_element_type=f32)


def dot_left(a, b):
    return lax.dot_general(a, b, (((0,), (0,)), ((), ())), preferred_element_type=f32)


def dot_right(a, b):
    return lax.dot_general(a, b, (((1,), (1,)), ((), ())), preferred_element_type=f32)


def row(ref):
    return ref[...].astype(f32)


def silu(x):
    h = 0.5 * x
    return h + h * jnp.tanh(h)


def silu_and_slope(x):
    h = 0.5 * x
    t = jnp.tanh(h)
    s = 0.5 + 0.5 * t
    act = h + h * t
    return act, s + act * (0.5 - 0.5 * t)


def tile_rows(count):
    for rows in (1024, 512, 256, 128):
        if count % rows == 0:
            return rows
    return count


def lane_masks(values, lanes):
    eye = lax.broadcasted_iota(i32, (lanes, lanes), 0) == lax.broadcasted_iota(i32, (lanes, lanes), 1)
    parts = []
    for start in range(0, values[0].shape[1], lanes):
        parts.append(
            jnp.concatenate(
                [jnp.where(eye, v[:, start : start + lanes], 0.0).astype(bf16) for v in values], axis=1
            )
        )
    ones = jnp.ones((lanes, lanes), bf16)
    zeros = jnp.zeros((lanes, lanes), bf16)
    if len(values) == 1:
        spread = ones
    else:
        spread = jnp.concatenate(
            [jnp.concatenate([ones, zeros], 1), jnp.concatenate([zeros, ones], 1)], 0
        )
    return dot(jnp.concatenate(parts, 0), spread)


def chosen_rows(rv, half, rows):
    low = jnp.where(rv >= half, rv - half, rv).astype(i16)
    iota = lax.broadcasted_iota(i32, (half, rows), 0).astype(i16)
    return jnp.where(iota == low, jnp.ones((), bf16), jnp.zeros((), bf16))


def forward_kernel(
    s_ref, ext_ref, el_hbm, rb_hbm, rv_ref, mk_ref, w1_ref, w2_ref, b2_ref, w3_ref, b3_ref, g_ref, b_ref,
    eo_hbm, p1_hbm, p2_hbm, ce_hbm, sum_ref,
    ts, rb, el, eo, p1, p2, ce, gb, qb, acc, pay, isem, osem,
    *, T, N, NB,
):
    L = el.shape[1]
    H = NB // 2

    def fetch(k, i):
        d = pl.ds(pl.multiple_of(i * T, T), T)
        v, hbm = ((rb, rb_hbm), (el, el_hbm))[k]
        return pltpu.make_async_copy(hbm.at[d], v.at[d], isem.at[k, i])

    def flush(i):
        d = pl.ds(pl.multiple_of(i * T, T), T)
        pairs = ((eo, eo_hbm), (p1, p1_hbm), (p2, p2_hbm), (ce, ce_hbm))
        return [pltpu.make_async_copy(v.at[d], h.at[d], osem.at[k, i]) for k, (v, h) in enumerate(pairs)]

    for i in range(N):
        for k in (0, 1):
            fetch(k, i).start()
    step = tile_rows(NB)

    def tables(j, _):
        d = pl.ds(pl.multiple_of(j * step, step), step)
        ts[d, :] = dot(ext_ref[d, :], w1_ref[L : 2 * L, :])
        return 0

    lax.fori_loop(0, 3 * NB // step, tables, 0)

    def gather(i):
        base = pl.multiple_of(i * T, T)
        for e in range(T):
            at = s_ref[i * (T // LANES) + e // LANES, e % LANES]
            gb[pl.ds(e, 1), :] = ts[pl.ds(at, 1), :] + rb[pl.ds(base + e, 1), :]

    def scatter(i):
        acc[...] += dot(chosen_rows(rv_ref[i], H, T), pay[...])

    def network(i):
        d = pl.ds(pl.multiple_of(i * T, T), T)
        latent = el[d, :]
        pre1 = dot(latent, w1_ref[:L, :]) + qb[...]
        p1[d, :] = pre1
        pre2 = dot(silu(pre1).astype(bf16), w2_ref[...]) + row(b2_ref)
        p2[d, :] = pre2
        pre3 = dot(silu(pre2).astype(bf16), w3_ref[...]) + row(b3_ref)
        center = pre3 - jnp.mean(pre3, axis=1, keepdims=True)
        ce[d, :] = center
        factor = lax.rsqrt(jnp.mean(center * center, axis=1, keepdims=True) + EPSILON)
        normed = center * factor * row(g_ref) + row(b_ref)
        rv = rv_ref[i]
        masks = lane_masks((mk_ref[i].astype(f32), (rv >= H).astype(f32)), L)
        message = normed * masks[:, :L]
        eo[d, :] = latent.astype(f32) + message
        rounded = message.astype(bf16)
        upper = rounded * masks[:, L:].astype(bf16)
        pay[...] = jnp.concatenate([rounded - upper, upper], axis=1)

    acc[...] = jnp.zeros_like(acc)
    pay[...] = jnp.zeros_like(pay)
    fetch(0, 0).wait()
    gather(0)
    qb[...] = gb[...]

    def body(i, _):
        fetch(1, i).wait()

        @pl.when(i + 1 < N)
        def _():
            fetch(0, i + 1).wait()

        scatter(jnp.maximum(i - 1, 0))
        gather(jnp.minimum(i + 1, N - 1))
        network(i)
        qb[...] = gb[...]
        for copy in flush(i):
            copy.start()
        return 0

    lax.fori_loop(0, N, body, 0)
    scatter(N - 1)
    sum_ref[:H, :] = acc[:, :L]
    sum_ref[H:, :] = acc[:, L:]

    def finish(i, _):
        for copy in flush(i):
            copy.wait()
        return 0

    lax.fori_loop(0, N, finish, 0)


def edge_forward(s, r, rb, ext, el, mask, weights, NB):
    E, L = el.shape
    T = tile_rows(E)
    N = E // T
    wide = jax.ShapeDtypeStruct((E, L), f32)
    whole = pltpu.VMEM((E, L), f32)
    tile = pltpu.VMEM((T, L), f32)
    return pl.pallas_call(
        functools.partial(forward_kernel, T=T, N=N, NB=NB),
        in_specs=[SMEM, VMEM, ANY, ANY, VMEM, VMEM] + [VMEM] * 7,
        out_specs=[ANY] * 4 + [VMEM],
        out_shape=[wide] * 4 + [jax.ShapeDtypeStruct((NB, L), f32)],
        scratch_shapes=[
            pltpu.VMEM((3 * NB, L), f32), whole, pltpu.VMEM((E, L), bf16),
            whole, whole, whole, whole, tile, tile,
            pltpu.VMEM((NB // 2, 2 * L), f32), pltpu.VMEM((T, 2 * L), bf16),
            pltpu.SemaphoreType.DMA((2, N)), pltpu.SemaphoreType.DMA((4, N)),
        ],
        compiler_params=pltpu.CompilerParams(vmem_limit_bytes=VMEM_BYTES),
        name="edge_forward",
    )(s, ext, el, rb, r.reshape(N, 1, T), mask.reshape(N, 1, T), *weights)


def remote(src, dst, send, recv, device):
    return pltpu.make_async_remote_copy(
        src_ref=src, dst_ref=dst, send_sem=send, recv_sem=recv, device_id=device, device_id_type=MESH
    )


def halo_kernel(
    nl_ref, s_ref, r_ref, w1_ref, b1_ref, ext_ref, sl_ref, rl_ref, rb_hbm, rb, tr, ri, send, recv, isem, osem, *, n, K, T
):
    NB, L = nl_ref.shape
    H = NB // 2
    C = H // K
    e, r = lax.axis_index("edges"), lax.axis_index("rep")
    h, x = r % 2, r // 2
    shared, other = 2 + x, 3 - x
    across = (e, (r + 2) % 4)
    peer, below, above = (e, r + 1 - 2 * h), (e - 1, r), (e + 1, r)
    has_below, has_above = e > 0, e < n - 1
    barrier = pltpu.get_barrier_semaphore()
    for device in (peer, across):
        pl.semaphore_signal(barrier, inc=1, device_id=device, device_id_type=MESH)

    @pl.when(has_below)
    def _():
        pl.semaphore_signal(barrier, inc=1, device_id=below, device_id_type=MESH)

    @pl.when(has_above)
    def _():
        pl.semaphore_signal(barrier, inc=1, device_id=above, device_id_type=MESH)

    sl_ref[...] = s_ref[...] - (e - 1) * NB
    rl_ref[...] = lax.rem(r_ref[...], NB)
    index = pltpu.make_async_copy(rl_ref, ri, isem)
    index.start()
    tr[...] = dot(nl_ref[...], w1_ref[2 * L :, :]) + row(b1_ref)
    ext_ref[NB : 2 * NB, :] = nl_ref[...]
    index.wait()
    pl.semaphore_wait(barrier, 2 + has_below.astype(i32) + has_above.astype(i32))

    def rows(start, c):
        return pl.ds(pl.multiple_of(start + h * H + c * C, 16), C)

    def to_above(c):
        return remote(nl_ref.at[rows(0, c)], ext_ref.at[rows(0, c)], send.at[0, c], recv.at[0, c], above)

    def to_below(c):
        return remote(nl_ref.at[rows(0, c)], ext_ref.at[rows(2 * NB, c)], send.at[1, c], recv.at[1, c], below)

    def pass_first(c):
        d = rows(0, c)
        return remote(ext_ref.at[d], ext_ref.at[d], send.at[2, c], recv.at[2, c], peer)

    def pass_last(c):
        d = rows(2 * NB, c)
        return remote(ext_ref.at[d], ext_ref.at[d], send.at[3, c], recv.at[3, c], peer)

    def cross_first(c):
        d = rows(0, c)
        return remote(ext_ref.at[d], ext_ref.at[d], send.at[4, c], recv.at[4, c], across)

    def cross_last(c):
        d = rows(2 * NB, c)
        return remote(ext_ref.at[d], ext_ref.at[d], send.at[5, c], recv.at[5, c], across)

    for c in (shared, 0, 1):

        @pl.when(has_above)
        def _():
            to_above(c).start()

        @pl.when(has_below)
        def _():
            to_below(c).start()

    @pl.when(jnp.logical_not(has_below))
    def _():
        ext_ref[:NB, :] = jnp.zeros((NB, L), ext_ref.dtype)

    @pl.when(jnp.logical_not(has_above))
    def _():
        ext_ref[2 * NB :, :] = jnp.zeros((NB, L), ext_ref.dtype)

    U = LANES

    def flush(i):
        d = pl.ds(pl.multiple_of(i * T, T), T)
        return pltpu.make_async_copy(rb.at[d], rb_hbm.at[d], osem.at[i])

    def tile(i, _):
        def rows_of(j, _):
            base = pl.multiple_of(i * T + j * U, U)
            for u in range(U):
                rb[pl.ds(base + u, 1), :] = tr[pl.ds(ri[base // LANES, u], 1), :]
            return 0

        lax.fori_loop(0, T // U, rows_of, 0)
        flush(i).start()
        return 0

    N = rb.shape[0] // T
    lax.fori_loop(0, N * 7 // 10, tile, 0)

    @pl.when(has_below)
    def _():
        to_above(shared).wait_recv()
        cross_first(shared).start()
        pass_first(shared).start()

    @pl.when(has_above)
    def _():
        to_below(shared).wait_recv()
        cross_last(shared).start()
        pass_last(shared).start()

    lax.fori_loop(N * 7 // 10, N, tile, 0)
    for c in (0, 1):

        @pl.when(has_below)
        def _():
            to_above(c).wait_recv()
            pass_first(c).start()

        @pl.when(has_above)
        def _():
            to_below(c).wait_recv()
            pass_last(c).start()

    @pl.when(has_below)
    def _():
        cross_first(other).wait_recv()
        pass_first(other).start()

    @pl.when(has_above)
    def _():
        cross_last(other).wait_recv()
        pass_last(other).start()

    for c in (shared, 0, 1):

        @pl.when(has_below)
        def _():
            to_below(c).wait_send()

        @pl.when(has_above)
        def _():
            to_above(c).wait_send()

    @pl.when(has_below)
    def _():
        cross_first(shared).wait_send()

    @pl.when(has_above)
    def _():
        cross_last(shared).wait_send()

    for c in range(K):

        @pl.when(has_below)
        def _():
            pass_first(c).wait()

        @pl.when(has_above)
        def _():
            pass_last(c).wait()

    def finish(i, _):
        flush(i).wait()
        return 0

    lax.fori_loop(0, N, finish, 0)


def halo_stage(nl, s, r, w1, b1, n):
    NB, L = nl.shape
    E = s.size
    T = tile_rows(E)
    flat = jax.ShapeDtypeStruct(s.shape, i32)
    sem = pltpu.SemaphoreType.DMA
    return pl.pallas_call(
        functools.partial(halo_kernel, n=n, K=4, T=T),
        in_specs=[VMEM] * 5,
        out_specs=[VMEM] * 3 + [ANY],
        out_shape=[jax.ShapeDtypeStruct((3 * NB, L), nl.dtype), flat, flat, jax.ShapeDtypeStruct((E, L), f32)],
        scratch_shapes=[
            pltpu.VMEM((E, L), f32), pltpu.VMEM((NB, L), f32), pltpu.SMEM(s.shape, i32),
            sem((6, 4)), sem((6, 4)), sem, sem((E // T,)),
        ],
        compiler_params=pltpu.CompilerParams(vmem_limit_bytes=VMEM_BYTES, collective_id=0, has_side_effects=True),
        name="halo",
    )(nl, s, r, w1, b1)


def node_kernel(
    part_ref, nl_ref, pm_ref, nc_ref, w1_ref, b1_ref, w2_ref, b2_ref, w3_ref, b3_ref, g_ref, b_ref,
    no_ref, rg_ref, mg_ref, gw1_ref, gw2_ref, gw3_ref, gv_ref,
    rbuf, xs, xr, sm, send, recv,
    *, K,
):
    NB, L = nl_ref.shape
    H = NB // 2
    C = H // K
    e, r = lax.axis_index("edges"), lax.axis_index("rep")
    h, x = r % 2, r // 2
    peer, across = (e, r + 1 - 2 * h), (e, (r + 2) % 4)
    barrier = pltpu.get_barrier_semaphore()
    for device in (peer, across):
        pl.semaphore_signal(barrier, inc=1, device_id=device, device_id_type=MESH)
    pl.semaphore_wait(barrier, 2)

    def at(half, c):
        return pl.ds(pl.multiple_of(half * H + c * C, C), C)

    def halves(c):
        return remote(part_ref.at[at(1 - h, c)], rbuf.at[pl.ds(c * C, C)], send.at[0, c], recv.at[0, c], peer)

    def exchange(c):
        d = pl.ds(pl.multiple_of(c * C, C), C)
        return remote(xs.at[d], xr.at[d], send.at[1, c], recv.at[1, c], across)

    def share(c):
        d = at(h, c)
        return remote(sm.at[d], sm.at[d], send.at[2, c], recv.at[2, c], peer)

    def arrived(c):
        d = at(1 - h, c)
        return remote(sm.at[d], sm.at[d], send.at[2, c], recv.at[2, c], peer)

    for c in range(K):
        halves(c).start()
    for c in range(K):
        halves(c).wait_recv()
        d = pl.ds(c * C, C)
        xs[d, :] = part_ref[at(h, c), :] + rbuf[d, :]
        exchange(c).start()
    for ref in (gw1_ref, gw2_ref, gw3_ref, gv_ref):
        ref[...] = jnp.zeros_like(ref)

    def body(q, _):
        c, mine = q // 2, q % 2 == 0
        half = jnp.where(mine, h, 1 - h)
        d = at(half, c)

        @pl.when(mine)
        def _():
            exchange(c).wait_recv()
            o = pl.ds(pl.multiple_of(c * C, C), C)
            sm[d, :] = (xs[o, :] + xr[o, :]).astype(bf16)
            share(c).start()

        @pl.when(jnp.logical_not(mine))
        def _():
            arrived(c).wait_recv()

        latent = nl_ref[d, :]
        inputs = jnp.concatenate([latent, sm[d, :]], axis=1)
        pre1 = dot(inputs, w1_ref[...]) + row(b1_ref)
        act1, slope1 = silu_and_slope(pre1)
        act1 = act1.astype(bf16)
        pre2 = dot(act1, w2_ref[...]) + row(b2_ref)
        act2, slope2 = silu_and_slope(pre2)
        act2 = act2.astype(bf16)
        pre3 = dot(act2, w3_ref[...]) + row(b3_ref)
        center = pre3 - jnp.mean(pre3, axis=1, keepdims=True)
        factor = lax.rsqrt(jnp.mean(center * center, axis=1, keepdims=True) + EPSILON)
        normed = center * factor
        keep = lane_masks((pm_ref[half * K + c].astype(f32),), L)
        no_ref[d, :] = latent.astype(f32) + keep * (normed * row(g_ref) + row(b_ref))
        cot = nc_ref[d, :]
        up = cot * keep
        inner = up * row(g_ref)
        g3 = factor * (
            inner
            - jnp.mean(inner, axis=1, keepdims=True)
            - normed * jnp.mean(inner * normed, axis=1, keepdims=True)
        )
        g3 = g3.astype(bf16)
        g2 = (dot_right(g3, w3_ref[...]) * slope2).astype(bf16)
        g1 = (dot_right(g2, w2_ref[...]) * slope1).astype(bf16)
        gin = dot_right(g1, w1_ref[...])
        rg_ref[d, :] = cot + gin[:, :L]
        mg_ref[d, :] = gin[:, L:]

        @pl.when(jnp.logical_and(mine, c * 2 // K == x))
        def _():
            gw3_ref[...] += dot_left(act2, g3)
            gw2_ref[...] += dot_left(act1, g2)
            gw1_ref[...] += dot_left(inputs, g1)
            sums = [jnp.sum(v.astype(f32), axis=0, keepdims=True) for v in (g1, g2, g3, up * normed, up)]
            gv_ref[...] += jnp.concatenate(sums + [jnp.zeros((3, L), f32)], axis=0)

        return 0

    lax.fori_loop(0, 2 * K, body, 0)
    for c in range(K):
        halves(c).wait_send()
        exchange(c).wait_send()
        share(c).wait_send()


def node_stage(partial, nl, mask, cot, weights):
    NB, L = nl.shape
    K = 4
    H = NB // 2
    rows = jax.ShapeDtypeStruct((NB, L), f32)
    square = jax.ShapeDtypeStruct((L, L), f32)
    return pl.pallas_call(
        functools.partial(node_kernel, K=K),
        in_specs=[VMEM] * 12,
        out_specs=[VMEM] * 7,
        out_shape=[rows, rows, rows, jax.ShapeDtypeStruct((2 * L, L), f32), square, square, jax.ShapeDtypeStruct((8, L), f32)],
        scratch_shapes=[
            pltpu.VMEM((H, L), f32), pltpu.VMEM((H, L), f32), pltpu.VMEM((H, L), f32), pltpu.VMEM((NB, L), bf16),
            pltpu.SemaphoreType.DMA((3, K)), pltpu.SemaphoreType.DMA((3, K)),
        ],
        compiler_params=pltpu.CompilerParams(vmem_limit_bytes=VMEM_BYTES, collective_id=1, has_side_effects=True),
        name="node_stage",
    )(partial, nl, mask.reshape(2 * K, 1, H // K), cot, *weights)


def backward_kernel(
    s_hbm, r_hbm, mg_ref, p1_hbm, p2_hbm, ce_hbm, el_hbm, ct_hbm, ni_hbm, rv_ref, mk_ref, w1_ref, w2_ref, w3_ref, g_ref,
    eg_hbm, no_hbm, gs_ref, gr_ref, gw1_ref, gw2_ref, gw3_ref, gv_ref,
    p1, p2, ce, el, ct, gb, qb, g1f, g1c, acc, pay, si, ri, nv, isem, osem, nsem, xsem, *sums,
    T, N, NB,
):
    L = el.shape[1]
    H = NB // 2
    Q = T // LANES

    def fetch(i):
        d = pl.ds(pl.multiple_of(i * T, T), T)
        pairs = ((p1, p1_hbm), (p2, p2_hbm), (ce, ce_hbm), (el, el_hbm), (ct, ct_hbm))
        return [pltpu.make_async_copy(h.at[d], v.at[d], isem.at[k, i]) for k, (v, h) in enumerate(pairs)]

    def flush(i):
        d = pl.ds(pl.multiple_of(i * T, T), T)
        return pltpu.make_async_copy(ct.at[d], eg_hbm.at[d], osem.at[i])

    for i in range(N):
        for copy in fetch(i):
            copy.start()
    into, out_of = pltpu.make_async_copy(ni_hbm, nv, nsem.at[0]), pltpu.make_async_copy(nv, no_hbm, nsem.at[1])
    into.start()
    index = [
        pltpu.make_async_copy(s_hbm, si.at[pl.ds(2 * Q, N * Q)], xsem.at[0]),
        pltpu.make_async_copy(s_hbm.at[pl.ds(0, Q)], si.at[pl.ds(Q, Q)], xsem.at[1]),
        pltpu.make_async_copy(r_hbm, ri.at[pl.ds(0, N * Q)], xsem.at[2]),
        pltpu.make_async_copy(r_hbm.at[pl.ds(0, Q)], ri.at[pl.ds(N * Q, Q)], xsem.at[3]),
    ]
    for copy in index:
        copy.start()
    for ref in (gw1_ref, gw2_ref, gw3_ref, gv_ref, acc, pay, g1c):
        ref[...] = jnp.zeros_like(ref)

    def clear(j, _):
        d = pl.ds(pl.multiple_of(j * 256, 256), 256)
        for a in sums:
            a[d, :] = jnp.zeros((256, L), f32)
        return 0

    lax.fori_loop(0, 3 * NB // 256, clear, 0)

    def gather(i):
        for e in range(T):
            gb[pl.ds(e, 1), :] = mg_ref[pl.ds(ri[i * Q + e // LANES, e % LANES], 1), :]

    def scatter(i):
        acc[...] += dot(chosen_rows(rv_ref[i], H, T), pay[...])

    def scatter_senders(i):
        for e in range(T):
            a = sums[e % len(sums)]
            at = pl.ds(si[(i + 2) * Q + e // LANES, e % LANES], 1)
            a[at, :] += g1c[pl.ds(e, 1), :]

    def network(i):
        d = pl.ds(pl.multiple_of(i * T, T), T)
        center = ce[d, :]
        factor = lax.rsqrt(jnp.mean(center * center, axis=1, keepdims=True) + EPSILON)
        normed = center * factor
        rv = rv_ref[i]
        masks = lane_masks((mk_ref[i].astype(f32), (rv >= H).astype(f32)), L)
        cot = ct[d, :]
        up = (cot + qb[...]) * masks[:, :L]
        inner = up * row(g_ref)
        g3 = factor * (
            inner
            - jnp.mean(inner, axis=1, keepdims=True)
            - normed * jnp.mean(inner * normed, axis=1, keepdims=True)
        )
        g3 = g3.astype(bf16)
        act2, slope2 = silu_and_slope(p2[d, :])
        gw3_ref[...] += dot_left(act2.astype(bf16), g3)
        g2 = (dot_right(g3, w3_ref[...]) * slope2).astype(bf16)
        act1, slope1 = silu_and_slope(p1[d, :])
        gw2_ref[...] += dot_left(act1.astype(bf16), g2)
        g1 = (dot_right(g2, w2_ref[...]) * slope1).astype(bf16)
        gw1_ref[...] += dot_left(el[d, :], g1)
        ct[d, :] = cot + dot_right(g1, w1_ref[:L, :])
        g1f[...] = g1.astype(f32)
        upper = g1 * masks[:, L:].astype(bf16)
        pay[...] = jnp.concatenate([g1 - upper, upper], axis=1)
        cols = [jnp.sum(v.astype(f32), axis=0, keepdims=True) for v in (g1, g2, g3, up * normed, up)]
        gv_ref[...] += jnp.concatenate(cols + [jnp.zeros((3, L), f32)], axis=0)

    for copy in index:
        copy.wait()
    gather(0)
    qb[...] = gb[...]

    def body(i, _):
        for copy in fetch(i):
            copy.wait()
        scatter(jnp.maximum(i - 1, 0))
        for e in range(T):
            line, lane = (i + 1) * Q + e // LANES, e % LANES
            gb[pl.ds(e, 1), :] = mg_ref[pl.ds(ri[line, lane], 1), :]
            a, spot = sums[e % len(sums)], pl.ds(si[line, lane], 1)
            a[spot, :] += g1c[pl.ds(e, 1), :]
        network(i)
        qb[...] = gb[...]
        g1c[...] = g1f[...]
        flush(i).start()
        return 0

    lax.fori_loop(0, N, body, 0)
    into.wait()
    out_of.start()
    scatter(N - 1)
    scatter_senders(N - 1)
    gr_ref[:H, :] = acc[:, :L]
    gr_ref[H:, :] = acc[:, L:]

    def merge(j, _):
        d = pl.ds(pl.multiple_of(j * 256, 256), 256)
        terms = [a[d, :] for a in sums]
        while len(terms) > 1:
            terms = [x + y for x, y in zip(terms[::2], terms[1::2])]
        gs_ref[d, :] = terms[0]
        return 0

    lax.fori_loop(0, 3 * NB // 256, merge, 0)

    def finish(i, _):
        flush(i).wait()
        return 0

    lax.fori_loop(0, N, finish, 0)
    out_of.wait()


def edge_backward(s, r, mg, p1, p2, ce, el, ct, no, mask, weights, NB):
    E, L = el.shape
    T = tile_rows(E)
    N = E // T
    whole = pltpu.VMEM((E, L), f32)
    tile = pltpu.VMEM((T, L), f32)
    square = jax.ShapeDtypeStruct((L, L), f32)
    return pl.pallas_call(
        functools.partial(backward_kernel, T=T, N=N, NB=NB),
        in_specs=[ANY, ANY, VMEM] + [ANY] * 6 + [VMEM] * 6,
        out_specs=[ANY] * 2 + [VMEM] * 6,
        out_shape=[
            jax.ShapeDtypeStruct((E, L), f32), jax.ShapeDtypeStruct((NB, L), f32),
            jax.ShapeDtypeStruct((3 * NB, L), f32), jax.ShapeDtypeStruct((NB, L), f32),
            square, square, square, jax.ShapeDtypeStruct((8, L), f32),
        ],
        scratch_shapes=[
            whole, whole, whole, pltpu.VMEM((E, L), bf16), whole, tile, tile, tile, tile,
            pltpu.VMEM((NB // 2, 2 * L), f32), pltpu.VMEM((T, 2 * L), bf16),
            pltpu.SMEM(((E + 2 * T) // LANES, LANES), i32), pltpu.SMEM(((E + T) // LANES, LANES), i32),
            pltpu.VMEM((NB, L), f32),
            pltpu.SemaphoreType.DMA((5, N)), pltpu.SemaphoreType.DMA((N,)), pltpu.SemaphoreType.DMA((2,)),
            pltpu.SemaphoreType.DMA((4,)),
        ]
        + [pltpu.VMEM((3 * NB, L), f32)] * ACCUMULATORS,
        compiler_params=pltpu.CompilerParams(vmem_limit_bytes=VMEM_BYTES),
        name="edge_backward",
    )(s, r, mg, p1, p2, ce, el, ct, no, r.reshape(N, 1, T), mask.reshape(N, 1, T), *weights)


def split_rows(value):
    high = value.astype(bf16)
    return jnp.concatenate([high, (value - high.astype(f32)).astype(bf16)], axis=1)


def tail_kernel(
    gs_ref, gr_ref, ext_ref, w1_ref, ew1_ref, ew2_ref, ew3_ref, ev_ref, nw1_ref, nw2_ref, nw3_ref, nv_ref,
    tot, pt_ref,
    hs, hr, ys, yr, ob, obr, xs, xr, pb, pr, ps, prs, ag, agf, send, recv, gsend, grecv, asend, arecv,
    *, n, K, R,
):
    L = gr_ref.shape[1]
    NB = gr_ref.shape[0]
    H = NB // 2
    C = H // K
    G = 2 * n
    PH = G * R
    e, r = lax.axis_index("edges"), lax.axis_index("rep")
    h, x = r % 2, r // 2
    me = x * n + e
    peer, across, below, above = (e, r + 1 - 2 * h), (e, (r + 2) % 4), (e - 1, r), (e + 1, r)
    has_below, has_above = e > 0, e < n - 1

    def member(k):
        j = (me + k) % G
        return j, (j % n, (j // n) * 2 + h)

    barrier = pltpu.get_barrier_semaphore()
    pl.semaphore_signal(barrier, inc=1, device_id=peer, device_id_type=MESH)

    def greet(k, _):
        pl.semaphore_signal(barrier, inc=1, device_id=member(k)[1], device_id_type=MESH)
        return 0

    lax.fori_loop(1, G, greet, 0)

    def twice(w):
        return jnp.concatenate([w, w], axis=1)

    ws = twice(w1_ref[L : 2 * L, :])
    wr = twice(w1_ref[2 * L :, :])

    def at(half, c):
        return pl.ds(pl.multiple_of(half * H + c * C, C), C)

    def halves(half, start=0):
        return pl.ds(pl.multiple_of(start + half * H, H), H)

    def own_block(half):
        return dot_right(split_rows(gs_ref[halves(half, NB), :]), ws) + dot_right(split_rows(gr_ref[halves(half), :]), wr)

    def pair_copy(k, c):
        return remote(hs.at[k, pl.ds(c * C, C)], hr.at[k, pl.ds(c * C, C)], send.at[k, c], recv.at[k, c], peer)

    def neighbour_copy(k, c):
        d = pl.ds(c * C, C)
        return remote(ys.at[k, d], yr.at[k, d], send.at[2 + k, c], recv.at[2 + k, c], below if k == 0 else above)

    own_copy = remote(ob, obr, send.at[4, 0], recv.at[4, 0], peer)

    def across_copy(c):
        d = pl.ds(c * C, C)
        return remote(xs.at[d], xr.at[d], send.at[5, c], recv.at[5, c], across)

    def total_copy(c):
        d = at(h, c)
        return remote(tot.at[d], tot.at[d], send.at[6, c], recv.at[6, c], peer)

    def total_arrived(c):
        d = at(1 - h, c)
        return remote(tot.at[d], tot.at[d], send.at[6, c], recv.at[6, c], peer)

    @pl.when(jnp.logical_not(has_above))
    def _():
        yr[0] = jnp.zeros((H, L), bf16)

    @pl.when(jnp.logical_not(has_below))
    def _():
        yr[1] = jnp.zeros((H, L), bf16)

    for k in (0, 1):
        hs[k] = gs_ref[halves(1 - h, 2 * NB * k), :].astype(bf16)

    pb[...] = jnp.zeros_like(pb)
    pb[:L, :] = ew1_ref[...]
    t = jnp.zeros((L, 2 * L), f32)
    for k in range(3):
        t += dot_left(ext_ref[k * NB : (k + 1) * NB, :], split_rows(gs_ref[k * NB : (k + 1) * NB, :]))
    pb[L : 2 * L, :] = t[:, :L] + t[:, L:]
    t = dot_left(ext_ref[NB : 2 * NB, :], split_rows(gr_ref[...]))
    pb[2 * L : 3 * L, :] = t[:, :L] + t[:, L:]
    o = 3 * L
    for ref in (ew2_ref, ew3_ref, ev_ref, nw1_ref, nw2_ref, nw3_ref, nv_ref):
        pb[o : o + ref.shape[0], :] = ref[...]
        o += ref.shape[0]

    def params_half(half):
        return pl.ds(pl.multiple_of(half * PH, 16), PH)

    params_pair = remote(pb.at[params_half(1 - h)], pr, asend.at[0], arecv.at[0], peer)
    pl.semaphore_wait(barrier, G)
    for c in range(K):
        for k in (0, 1):
            pair_copy(k, c).start()
    params_pair.start()
    for c in range(K):
        d = pl.ds(c * C, C)
        for k in (0, 1):
            pair_copy(k, c).wait_recv()
            ys[k, d, :] = (gs_ref[at(h, c + 2 * k * NB // C), :] + hr[k, d, :].astype(f32)).astype(bf16)

        @pl.when(has_below)
        def _():
            neighbour_copy(0, c).start()

        @pl.when(has_above)
        def _():
            neighbour_copy(1, c).start()

    params_pair.wait_recv()
    ps[...] = (pb[params_half(h), :] + pr[...]).astype(bf16)

    def share_rows(j):
        return pl.ds(pl.multiple_of(j * R, 16), R)

    def spread(k):
        j, device = member(k)
        return remote(ps.at[share_rows(j)], prs.at[share_rows(me)], gsend.at[0, k], grecv.at[0, me], device)

    def spread_arrived(k):
        j, device = member(k)
        return remote(ps.at[share_rows(j)], prs.at[share_rows(j)], gsend.at[0, k], grecv.at[0, j], device)

    def collect(k):
        j, device = member(k)
        return remote(ag.at[share_rows(me)], ag.at[share_rows(me)], gsend.at[1, k], grecv.at[1, me], device)

    def collect_arrived(k):
        j, device = member(k)
        return remote(ag.at[share_rows(j)], ag.at[share_rows(j)], gsend.at[1, k], grecv.at[1, j], device)

    def start_spread(k, _):
        spread(k).start()
        return 0

    lax.fori_loop(1, G, start_spread, 0)

    def neighbours(c):
        d = pl.ds(c * C, C)

        @pl.when(has_above)
        def _():
            neighbour_copy(0, c).wait_recv()

        @pl.when(has_below)
        def _():
            neighbour_copy(1, c).wait_recv()

        both = yr[0, d, :].astype(f32) + yr[1, d, :].astype(f32)
        xs[d, :] = (tot[at(h, c), :] + dot_right(split_rows(both), ws)).astype(bf16)
        across_copy(c).start()

    def finish(c):
        d = pl.ds(c * C, C)
        across_copy(c).wait_recv()
        tot[at(h, c), :] = xs[d, :].astype(f32) + xr[d, :].astype(f32)
        total_copy(c).start()

    ob[...] = own_block(1 - h)
    own_copy.start()
    tot[halves(h), :] = own_block(h)
    own_copy.wait_recv()
    tot[halves(h), :] += obr[...]
    for c in range(K // 2):
        neighbours(c)

    def add_share(k, total):
        spread_arrived(k).wait_recv()
        return total + prs[share_rows(member(k)[0]), :].astype(f32)

    ag[share_rows(me), :] = lax.fori_loop(1, G, add_share, ps[share_rows(me), :].astype(f32)).astype(bf16)

    def start_collect(k, _):
        collect(k).start()
        return 0

    lax.fori_loop(1, G, start_collect, 0)
    for c in range(K // 2, K):
        neighbours(c)
    for c in range(K):
        finish(c)

    def end_collect(k, _):
        collect_arrived(k).wait_recv()
        return 0

    lax.fori_loop(1, G, end_collect, 0)
    params_all = remote(ag, agf, asend.at[1], arecv.at[1], peer)
    params_all.start()
    pt_ref[params_half(h), :] = ag[...].astype(f32)
    for c in range(K):
        total_arrived(c).wait_recv()
    params_all.wait_recv()
    pt_ref[params_half(1 - h), :] = agf[...].astype(f32)

    def end_sends(k, _):
        spread(k).wait_send()
        collect(k).wait_send()
        return 0

    lax.fori_loop(1, G, end_sends, 0)
    own_copy.wait_send()
    params_pair.wait_send()
    params_all.wait_send()
    for c in range(K):
        pair_copy(0, c).wait_send()
        pair_copy(1, c).wait_send()
        across_copy(c).wait_send()
        total_copy(c).wait_send()

        @pl.when(has_below)
        def _():
            neighbour_copy(0, c).wait_send()

        @pl.when(has_above)
        def _():
            neighbour_copy(1, c).wait_send()


def tail_stage(gs, gr, ext, w1, parts, n):
    NB, L = gr.shape
    H, K, G = NB // 2, 4, 2 * n
    count = 2 * L + sum(p.shape[0] for p in parts)
    R = -(-count // (2 * G * 16)) * 16
    PH = G * R
    half = lambda kind: pltpu.VMEM((H, L), kind)
    two = lambda kind: pltpu.VMEM((2, H, L), kind)
    par = lambda kind: pltpu.VMEM((PH, L), kind)
    sem = pltpu.SemaphoreType.DMA
    return pl.pallas_call(
        functools.partial(tail_kernel, n=n, K=K, R=R),
        in_specs=[VMEM] * (4 + len(parts)),
        out_specs=[VMEM] * 2,
        out_shape=[jax.ShapeDtypeStruct((NB, L), f32), jax.ShapeDtypeStruct((2 * PH, L), f32)],
        scratch_shapes=[
            two(bf16), two(bf16), two(bf16), two(bf16), half(f32), half(f32), half(bf16), half(bf16),
            pltpu.VMEM((2 * PH, L), f32), par(f32), par(bf16), par(bf16), par(bf16), par(bf16),
            sem((7, K)), sem((7, K)), sem((2, G)), sem((2, G)), sem((2,)), sem((2,)),
        ],
        compiler_params=pltpu.CompilerParams(vmem_limit_bytes=VMEM_BYTES, collective_id=2, has_side_effects=True),
        name="tail",
    )(gs, gr, ext, w1, *parts)


def finish_kernel(tot_ref, rg_ref, pt_ref, ng_ref, *outs):
    ng_ref[...] = rg_ref[...] + tot_ref[...]
    L = tot_ref.shape[1]
    first, after = 3 * L + 2 * L, 3 * L + 2 * L + 8
    second = after + 4 * L
    spots = [
        (0, 3 * L), first, (3 * L, L), first + 1, (4 * L, L), first + 2, first + 3, first + 4,
        (after, 2 * L), second, (after + 2 * L, L), second + 1, (after + 3 * L, L), second + 2, second + 3, second + 4,
    ]
    for out, spot in zip(outs, spots):
        if isinstance(spot, tuple):
            out[...] = pt_ref[spot[0] : spot[0] + spot[1], :]
        else:
            out[...] = pt_ref[spot, :]


def finish_stage(tot, rg, pt):
    L = tot.shape[1]
    mat = lambda k: jax.ShapeDtypeStruct((k * L, L), f32)
    vec = jax.ShapeDtypeStruct((L,), f32)
    shapes = [mat(3), vec, mat(1), vec, mat(1), vec, vec, vec, mat(2), vec, mat(1), vec, mat(1), vec, vec, vec]
    return pl.pallas_call(
        finish_kernel,
        in_specs=[VMEM] * 3,
        out_specs=[VMEM] * 17,
        out_shape=[jax.ShapeDtypeStruct(tot.shape, f32)] + shapes,
        compiler_params=pltpu.CompilerParams(vmem_limit_bytes=VMEM_BYTES),
        name="finish",
    )(tot, rg, pt)


def shards(
    node_latent, edge_latent, senders, receivers, edge_mask, particle_mask,
    edge_lift, lifting, edge_middle, mixing, edge_final, closing, stretch, offset,
    node_first, opening, node_second, turning, node_third, ending, dilate, displace,
    node_cotangent, edge_cotangent,
):
    NB, L = node_latent.shape
    vec = lambda v: v.reshape(1, L)
    n = lax.axis_size("edges")
    ext, s, r, rb = halo_stage(node_latent, senders.reshape(-1, LANES), receivers.reshape(-1, LANES), edge_lift, vec(lifting), n)
    eo, p1, p2, ce, partial = edge_forward(
        s, r, rb, ext, edge_latent, edge_mask,
        (edge_lift, edge_middle, vec(mixing), edge_final, vec(closing), vec(stretch), vec(offset)), NB,
    )
    no, rg, mg, nw1, nw2, nw3, nv = node_stage(
        partial, node_latent, particle_mask, node_cotangent,
        (node_first, vec(opening), node_second, vec(turning), node_third, vec(ending), vec(dilate), vec(displace)),
    )
    eg, no, gs, gr, ew1, ew2, ew3, ev = edge_backward(
        s, r, mg, p1, p2, ce, edge_latent, edge_cotangent, no, edge_mask,
        (edge_lift, edge_middle, edge_final, vec(stretch)), NB,
    )
    path, totals = tail_stage(gs, gr, ext, edge_lift, (ew1, ew2, ew3, ev, nw1, nw2, nw3, nv), n)
    node_grad, *grads = finish_stage(path, rg, totals)
    return (no, eo, node_grad, eg, *grads)


def solution(mesh):
    node, edge, flat = P("edges", None), P(("edges", "rep"), None), P(("edges", "rep"))
    in_specs = (node, edge, flat, flat, flat, P("edges")) + (P(),) * 16 + (node, edge)
    out_specs = (node, edge, node, edge) + (P(),) * 16
    return jax.shard_map(shards, mesh=mesh, in_specs=in_specs, out_specs=out_specs, check_vma=False)
```
